128 devices in a mesh: lb: 16 (over z_lo, y, core), rb: 8 (over x, z_hi).
Axes of the slice: x: 4, y: 4, z: 4 (z_hi: 2, z_lo: 2; z = z_hi * 2 + z_lo), core: 2. Of those that a mesh axis runs over, the one named last changes fastest.
Arguments:
- wavefunction: bfloat16 [3072, 4, 3072], P('lb', None, 'rb'), may hold values from -6 to 6
- left_environment: bfloat16 [8, 2048, 3072], P(None, 'lb'), may hold values from -0.109375 to 0.109375
- operator_left: float32 [8, 8, 2, 2], replicated, may hold values from -1.5 to 1.5
- operator_right: float32 [8, 8, 2, 2], replicated, may hold values from -1.5 to 1.5
- right_environment: bfloat16 [8, 3072, 3072], P(None, 'rb', 'lb'), may hold values from -0.0546875 to 0.0546875
- row_sector: int32 [16], replicated, may hold values from 0 to 7, never falling along the last dimension, each value on 1 to 4 neighbouring positions
Outputs:
- applied_state: bfloat16 [2048, 4, 3072], P('lb', None, 'rb')
- density: float32 [2048, 2048], P('lb', 'rb')
The draws below stay inside these ranges and needn't reach their ends.
Inputs may be any that keep to these rules, and one draw needn't show every extreme that they name: `row_sector`: entry t is the sector of output rows t * 128 to (t + 1) * 128 - 1. Entries never fall along t; each sector holds 1 to 4 tiles, and one holds exactly 4.
All inputs are finite; a program needn't handle non-finite values.
Results may differ from the reference program's by a relative error of at most 0.013.
Values may be sent and summed in bfloat16 or wider, within the bound.
A program may use at most 128 MiB of HBM per device.

```python
import math
import jax
import jax.numpy as jnp
import numpy as np
from jax import lax

BOND_WIDTH = 3072
CHANNELS = 8
ROW_DEV = 128
SECTOR_TILES = 4
TILES = 16
ROWS = 2048
SECTORS = 8


def raised(values, rng, source, target, blocks, factor):
    owner, partner = [(jnp.arange(values.shape[position]) // (values.shape[position] // blocks)).reshape([-1 if axis == position else 1 for axis in range(values.ndim)]) for position in (source, target)]
    chosen = jax.random.permutation(rng, blocks)[partner]
    strong = (owner == chosen) | (owner == (partner + blocks // 2) % blocks)
    return jnp.where(strong, factor * values, values)


def steps_of(key, dims, cuts, least, high):
    factor_of, own = 1.0, jax.random.fold_in(key, 6)
    for axis_at, shards_of in cuts:
        heights = jnp.exp(jax.random.uniform(jax.random.fold_in(own, axis_at), (shards_of,), jnp.float32, least / len(cuts), high / len(cuts)))
        factor_of = factor_of * jnp.repeat(heights, dims[axis_at] // shards_of).reshape([-1 if axis == axis_at else 1 for axis in range(len(dims))])
    return factor_of


def profile(number_of, total, reach, lean):
    portions = [(1 << 20) // math.isqrt(standing ** lean) + 1 for standing in range(2, number_of + 1)]
    rest, given = total - reach - (number_of - 1), [1] * (number_of - 1)
    while rest > 0:
        candidates = [i for i in range(number_of - 1) if given[i] < reach]
        whole, left = sum([portions[i] for i in candidates]), rest
        for i in candidates:
            more = min(reach - given[i], max(1, left * portions[i] // whole), rest)
            given[i] = given[i] + more
            rest = rest - more
    return np.array([reach] + given)


def uneven_parts(key, number_of, total, most, lean):
    if number_of == 2:
        one = jax.random.randint(key, (), max(1, total - most), min(most, total - 1) + 1)
        return jnp.stack([one, total - one])
    tallies = jnp.asarray(profile(number_of, total, most, lean), jnp.int32)
    couples = (number_of - 1) // 2
    source_of, taker = tallies[1:1 + 2 * couples:2], tallies[2:2 + 2 * couples:2]
    margin = jnp.minimum(source_of - 1, most - taker)
    passed = jax.random.randint(jax.random.fold_in(key, 1), (couples,), 0, 1 << 20) % (margin + 1)
    tallies = tallies.at[1:1 + 2 * couples:2].set(source_of - passed).at[2:2 + 2 * couples:2].set(taker + passed)
    return tallies[jax.random.permutation(jax.random.fold_in(key, 2), number_of)]


def centred(stream_key, dims, deviation, limit, split=(), dtype=jnp.bfloat16):
    factor_of = steps_of(stream_key, dims, split, -0.22, 0.18) if split else 1.0
    drawn = jax.random.normal(stream_key, dims, jnp.float32) * deviation * factor_of
    return jnp.minimum(jnp.maximum(drawn, -limit), limit).astype(dtype)


def bell_draw_with(stream_key, shape, width, reach, shards, heavy, held_as=jnp.bfloat16):
    entries = width * jax.random.normal(stream_key, shape, jnp.float32)
    if shards:
        entries = entries * steps_of(stream_key, shape, shards, -0.22, 0.18)
    return jnp.clip(raised(entries, jax.random.fold_in(stream_key, 3), *heavy), -reach, reach).astype(held_as)


def setup_inputs(seed: int = 0) -> dict:
    streams_of = jax.random.split(jax.random.key(seed), 7)
    wavefunction = centred(streams_of[0], (BOND_WIDTH, 4, BOND_WIDTH), 1.0, 6.0, ((0, 16), (2, 8)))
    left_environment = centred(streams_of[1], (CHANNELS, ROWS, BOND_WIDTH), BOND_WIDTH ** -0.5, 0.109375, ((1, 16),))
    operator_left = centred(streams_of[2], (CHANNELS, CHANNELS, 2, 2), (2 * CHANNELS) ** -0.5, 1.5, (), jnp.float32)
    operator_right = centred(streams_of[3], (CHANNELS, CHANNELS, 2, 2), (2 * CHANNELS) ** -0.5, 1.5, (), jnp.float32)
    right_environment = bell_draw_with(streams_of[4], (CHANNELS, BOND_WIDTH, BOND_WIDTH), (CHANNELS * BOND_WIDTH) ** -0.5, 0.0546875, ((1, 8), (2, 16)), (1, 2, 16, 2.0))
    row_sector = jnp.searchsorted(jnp.cumsum(uneven_parts(streams_of[5], SECTORS, TILES, SECTOR_TILES, 0)), jnp.arange(TILES), side="right").astype(jnp.int32)
    return dict(wavefunction=wavefunction, left_environment=left_environment, operator_left=operator_left, operator_right=operator_right, right_environment=right_environment, row_sector=row_sector)


def combine_operators(operator_left, operator_right):
    channels = operator_left.shape[0]
    joined = jnp.einsum('aups,uvqt->avpqst', operator_left, operator_right, precision=lax.Precision.HIGHEST)
    return joined.reshape(channels, channels, 4, 4)

def reference(wavefunction, left_environment, operator_left, operator_right, right_environment, row_sector):
    combined = combine_operators(operator_left, operator_right)
    state_matrix = wavefunction.reshape(BOND_WIDTH, 4 * BOND_WIDTH)
    right_matrix = right_environment.reshape(CHANNELS * BOND_WIDTH, BOND_WIDTH)
    blocks = left_environment.reshape(CHANNELS, TILES, ROW_DEV, BOND_WIDTH).transpose(1, 0, 2, 3)

    def apply_block(left_block):
        left_part = jnp.dot(left_block.reshape(CHANNELS * ROW_DEV, BOND_WIDTH), state_matrix, preferred_element_type=jnp.float32)
        left_part = left_part.reshape(CHANNELS, ROW_DEV, 4, BOND_WIDTH)
        mixed_part = jnp.einsum('avyx,alxr->lyvr', combined, left_part, precision=lax.Precision.HIGHEST).astype(jnp.bfloat16)
        result = jnp.dot(mixed_part.reshape(ROW_DEV * 4, CHANNELS * BOND_WIDTH), right_matrix, preferred_element_type=jnp.float32)
        return result.astype(jnp.bfloat16).reshape(ROW_DEV, 4, BOND_WIDTH)
    applied = lax.map(apply_block, blocks).reshape(ROWS, 4, BOND_WIDTH)
    flat = applied.reshape(ROWS, 4 * BOND_WIDTH)
    gram = jnp.dot(flat, flat.T, preferred_element_type=jnp.float32)
    tile_labels = jnp.repeat(row_sector, ROW_DEV)
    same_sector = tile_labels[:, None] == tile_labels[None, :]
    density = jnp.where(same_sector, gram, jnp.float32(0.0)) * (1.0 / math.sqrt(4.0 * BOND_WIDTH))
    return (applied, density)
```

```python
import functools
import math

import jax
import jax.numpy as jnp
from jax import lax
from jax.experimental import pallas as pl
from jax.experimental.pallas import tpu as pltpu
from jax.sharding import Mesh
from jax.sharding import PartitionSpec as P

BOND_WIDTH = 3072
SECTOR_TILES = 4
AXES = ("zl", "y", "core", "x", "zh")
LB = ("zl", "y", "core")
RB = ("x", "zh")
BF16, F32 = jnp.bfloat16, jnp.float32

MAIN, REST = 128, 64
PIECES = (
    (("z", 1, 0, 64), ("z", -1, 64, 48), ("y", 1, 112, 32), ("y", -1, 144, 48)),
    (("z", 1, 0, 32), ("z", -1, 32, 32), ("y", 1, 64, 32), ("y", -1, 96, 32)),
    (("z", 1, 0, 32), ("z", -1, 32, 16), ("y", -1, 48, 16)),
)
UNIT_BYTES = (1536 * 2, 8 * 384 * 2, 8 * 384 * 2)
SHARD = (192, MAIN, REST)
SOURCES = tuple((dz, dy) for dz in (0, 1) for dy in range(4))
MESSAGES = tuple(
    (phase, piece, source)
    for phase in range(3)
    for piece in range(len(PIECES[phase]))
    for source in SOURCES[1:]
)


def forwards(phase, piece, source):
    tree, turn = PIECES[phase][piece][:2]
    (dz, dy), on, back = source, "+-"[turn < 0], (-turn) % 4
    named = lambda link, place: (link, (phase, piece, place))
    if tree == "z":
        if source == (1, 0):
            return [named("+", (1, 3)), named("-", (1, 1))]
        return [named(on, (dz, 2))] if dy == back else []
    if dz:
        return []
    across = [named("z", (1, dy))]
    return [named(on, (0, 2)), *across] if dy == back else across


def own_sends():
    for phase in range(3):
        pieces = range(len(PIECES[phase]))
        for piece in sorted(pieces, key=lambda p: PIECES[phase][p][0] == "y"):
            yield "z", (phase, piece, (1, 0))
        for piece in sorted(pieces, key=lambda p: PIECES[phase][p][0] == "z"):
            yield "+", (phase, piece, (0, 3))
            yield "-", (phase, piece, (0, 1))


def schedule(rate=43.5e3, lag=1.0, lead=5.0, step=0.05):
    spent = {"first": 3.0, "mix": 1.6, "second": (None, 1.6, 1.3)}
    waiting = {link: [] for link in "+-z"}
    for order, (link, message) in enumerate(own_sends()):
        waiting[link].append((message[0], order, message, True))
    free_at = dict.fromkeys("+-z", 0.0)
    arriving, beside, done, ops, issued = [], [], set(), [], []
    pieces_left = {(p, s): len(PIECES[p]) for p in range(3) for s in SOURCES[1:]}
    ready = {(p, s): None for p in range(3) for s in SOURCES}
    for phase in range(3):
        ready[phase, (0, 0)] = 4.0 + phase
    firsts, mixes, seconds = 0, 0, [0, 0]
    order, now, tc_free = 1000, 0.0, 0.0
    while seconds[1] < 8:
        now += step
        for link in "+-z":
            if free_at[link] <= now and waiting[link]:
                job = min(waiting[link])
                waiting[link].remove(job)
                phase, piece, _ = message = job[2]
                took = PIECES[phase][piece][3] * UNIT_BYTES[phase] / rate
                if job[3]:
                    issued.append((max(0.0, now - lead), len(issued), link, message))
                free_at[link] = now + took
                arriving.append((now + took + lag, message))
        if tc_free > now:
            continue
        landed = [entry for entry in arriving if entry[0] <= now]
        if landed:
            entry = min(landed)
            arriving.remove(entry)
            message = entry[1]
            onward = forwards(*message)
            for link, passed in onward:
                order += 1
                waiting[link].append((passed[0], order, passed, False))
            ops.append((now, "take", message, onward))
            phase, _, source = message
            pieces_left[phase, source] -= 1
            if not pieces_left[phase, source]:
                ops.append((now, "share", phase, source))
                size = SHARD[phase] * UNIT_BYTES[phase]
                ready[phase, source] = now + 2.0 + size / 400e3
            tc_free = now + 0.2
            continue
        able = [k for k, at in ready.items() if at is not None and at <= now and k not in done]
        able = [k for k in able if k[0] == 0 or mixes == 4]
        if firsts == 8 and mixes < 4:
            ops.append((now, "mix", mixes))
            mixes += 1
            tc_free = now + spent["mix"]
        elif able:
            phase, source = min(able, key=lambda k: (k[0], ready[k]))
            done.add((phase, source))
            if phase == 0:
                ops.append((now, "first", source, firsts == 0))
                firsts += 1
                tc_free = now + spent["first"]
            else:
                ops.append((now, "second", phase, source))
                seconds[phase - 1] += 1
                tc_free = now + spent["second"][phase]
                if seconds[phase - 1] == 8:
                    ops.append((tc_free, "sum", phase))
    for at, _, link, message in reversed(issued):
        place = next((i for i, op in enumerate(ops) if op[0] > at), len(ops))
        ops.insert(place, (at, "send", link, message))
    return [op[1:] for op in ops], now


def ring(value, by, size):
    return lax.rem(value + (by % size), size)


def kernel(
    ops, w_ref, l_ref, r_ref, comb_ref, out_ref,
    left, wide, main, rest, acc, mixed, coef, part_main, part_rest, from_main, from_rest,
    kept_main, kept_rest, away_main, away_rest, back_main, back_rest,
    local_sem, send_sem, recv_sem, share_send, share_recv, x_send, x_recv, z_send, z_recv,
):
    zl, y, core, x, zh = (lax.axis_index(a) for a in AXES)
    gathered = (wide, main, rest)
    number = {m: i for i, m in enumerate(MESSAGES)}
    neighbour = {
        "+": {"y": ring(y, 1, 4)},
        "-": {"y": ring(y, -1, 4)},
        "z": {"zl": 1 - zl},
    }
    mesh_type = pl.DeviceIdType.MESH

    def chip(source):
        dz, dy = source
        return (1 - zl if dz else zl) * 4 + ring(y, dy, 4)

    barrier = pltpu.get_barrier_semaphore()
    partners = [*neighbour.values(), {"core": 1 - core}, {"zh": 1 - zh}]
    partners += [{"x": ring(x, by, 4)} for by in (1, 2, 3)]
    for partner in partners:
        pl.semaphore_signal(barrier, inc=1, device_id=partner, device_id_type=mesh_type)

    here = chip((0, 0)) * 2 + core
    loads = [
        pltpu.make_async_copy(w_ref, wide.at[here], local_sem.at[0]),
        pltpu.make_async_copy(r_ref.at[:, 0:MAIN], main.at[here], local_sem.at[1]),
        pltpu.make_async_copy(r_ref.at[:, MAIN : MAIN + REST], rest.at[here], local_sem.at[2]),
        pltpu.make_async_copy(l_ref, left, local_sem.at[3]),
    ]
    for load in loads:
        load.start()
    row = lax.broadcasted_iota(jnp.int32, (256, 32), 0)
    column = lax.broadcasted_iota(jnp.int32, (256, 32), 1)
    spread = (row // 8 == column).astype(BF16)
    row = lax.broadcasted_iota(jnp.int32, (256, 256), 0)
    column = lax.broadcasted_iota(jnp.int32, (256, 256), 1)
    same = row % 8 == column % 8
    high = comb_ref[...].astype(BF16)
    low = (comb_ref[...] - high.astype(F32)).astype(BF16)
    for at, term in enumerate((high, low)):
        tall = jnp.dot(spread, term, preferred_element_type=F32).astype(BF16)
        full = lax.dot_general(tall, spread, (((1,), (1,)), ((), ())), preferred_element_type=F32)
        coef[at * 256 : at * 256 + 256] = jnp.where(same, full, 0.0).astype(BF16)
    pl.semaphore_wait(barrier, len(partners))
    for load in loads:
        load.wait()

    sent = []

    def piece_of(message, receiver):
        phase, piece, _ = message
        start, size = PIECES[phase][piece][2:]
        if phase == 0:
            return wide.at[receiver, pl.ds(start, size)]
        return gathered[phase].at[receiver, :, pl.ds(start, size)]

    def send(link, message, source):
        block = piece_of(message, chip(source) * 2 + core)
        at = number[message]
        copy = pltpu.make_async_remote_copy(
            block, block, send_sem.at[at], recv_sem.at[at],
            device_id=neighbour[link], device_id_type=mesh_type,
        )
        copy.start()
        sent.append(copy)

    def arrived(message):
        block = piece_of(message, chip(message[2]) * 2 + core)
        at = number[message]
        pltpu.make_async_remote_copy(
            block, block, send_sem.at[at], recv_sem.at[at],
            device_id=neighbour["z"], device_id_type=mesh_type,
        ).wait_recv()

    def share(phase, source, owner):
        at = phase * 8 + SOURCES.index(source)
        block = gathered[phase].at[chip(source) * 2 + owner]
        return pltpu.make_async_remote_copy(
            block, block, share_send.at[at], share_recv.at[at],
            device_id={"core": 1 - core}, device_id_type=mesh_type,
        )

    def first(source, fresh):
        k = chip(source)
        columns = pl.ds(pl.multiple_of(k * 384, 384), 384)

        @pl.loop(0, 6)
        def _(tile):
            lanes = pl.ds(pl.multiple_of(tile * 256, 256), 256)
            block = wide[pl.ds(k * 2, 2), :, lanes].reshape(384, 256)
            product = jnp.dot(left[:, columns], block, preferred_element_type=F32)
            if fresh:
                acc[:, lanes] = product
            else:
                acc[:, lanes] += product

    def mix(quarter):
        @pl.loop(quarter * 2, quarter * 2 + 2)
        def _(group):
            halves = []
            for sub in range(2):
                start = pl.multiple_of(group * 16 + sub * 8, 8)
                stack = jnp.concatenate(
                    [
                        acc[pl.ds(a * 128 + start, 8), s * 384 : s * 384 + 384]
                        for a in range(8)
                        for s in range(4)
                    ],
                    axis=0,
                )
                top = stack.astype(BF16)
                under = (stack - top.astype(F32)).astype(BF16)
                both = jnp.dot(coef[...], top, preferred_element_type=F32)
                third = jnp.dot(coef[0:256], under, preferred_element_type=F32)
                halves.append(both[0:256] + both[256:512] + third)
            for v in range(8):
                for out_site in range(4):
                    at = (v * 4 + out_site) * 8
                    value = jnp.concatenate([h[at : at + 8] for h in halves], axis=0)
                    rows = pl.ds(pl.multiple_of(out_site * 128 + group * 16, 16), 16)
                    mixed[rows, v * 384 : v * 384 + 384] = value.astype(BF16)

    parts, froms = (None, part_main, part_rest), (None, from_main, from_rest)
    keeps, aways, backs = (None, kept_main, kept_rest), (None, away_main, away_rest), (None, back_main, back_rest)

    def to_owner(phase, k):
        owner, half = k // 2, lax.rem(k, 2)
        slot = lax.rem(x - owner + 7, 4)
        slot = jnp.minimum(slot, 2)
        copy = pltpu.make_async_remote_copy(
            parts[phase].at[k], froms[phase].at[half, slot],
            x_send.at[(phase - 1) * 8 + k], x_recv.at[(phase - 1) * 6 + half * 3 + slot],
            device_id={"x": owner}, device_id_type=mesh_type,
        )
        return copy, x != owner

    def second(phase, source):
        k = chip(source)
        width = 2 * SHARD[phase]

        @pl.loop(0, 4)
        def _(tile):
            rows = pl.ds(pl.multiple_of(tile * 128, 128), 128)
            total = None
            for v in range(8):
                block = gathered[phase][pl.ds(k * 2, 2), v].reshape(width, 384)
                product = lax.dot_general(
                    mixed[rows, v * 384 : v * 384 + 384], block,
                    (((1,), (1,)), ((), ())), preferred_element_type=F32,
                )
                total = product if total is None else total + product
            parts[phase][k, rows] = total.astype(BF16)

        copy, away = to_owner(phase, k)

        @pl.when(away)
        def _():
            copy.start()

    def z_copy(phase):
        return pltpu.make_async_remote_copy(
            aways[phase], backs[phase], z_send.at[phase - 1], z_recv.at[phase - 1],
            device_id={"zh": 1 - zh}, device_id_type=mesh_type,
        )

    def sum_x(phase, half, put):
        for slot in range(3):
            pltpu.make_async_remote_copy(
                parts[phase].at[0], froms[phase].at[half, slot],
                x_send.at[0], x_recv.at[(phase - 1) * 6 + half * 3 + slot],
                device_id={"x": ring(x, 1, 4)}, device_id_type=mesh_type,
            ).wait_recv()

        @pl.loop(0, 8)
        def _(tile):
            rows = pl.ds(pl.multiple_of(tile * 64, 64), 64)
            total = parts[phase][x * 2 + half, rows].astype(F32)
            for slot in range(3):
                total += froms[phase][half, slot, rows].astype(F32)
            put(rows, total)

    def sum_parts(phase):
        def put_away(rows, total):
            aways[phase][rows] = total.astype(BF16)

        def put_kept(rows, total):
            keeps[phase][rows] = total

        sum_x(phase, 1 - zh, put_away)
        z_copy(phase).start()
        sum_x(phase, zh, put_kept)

    def finish(phase):
        z_copy(phase).wait_recv()
        start, width = (0, 2 * MAIN) if phase == 1 else (2 * MAIN, 2 * REST)
        for site in range(4):
            rows = slice(site * 128, site * 128 + 128)
            value = keeps[phase][rows] + backs[phase][rows].astype(F32)
            out_ref[site, :, start : start + width] = value.astype(BF16)

    for phase in range(3):
        share(phase, (0, 0), core).start()
    for op in ops:
        if op[0] == "send":
            send(op[1], op[2], (0, 0))
        elif op[0] == "take":
            arrived(op[1])
            for link, passed in op[2]:
                send(link, passed, op[1][2])
        elif op[0] == "share":
            share(op[1], op[2], core).start()
        elif op[0] == "first":
            share(0, op[1], 1 - core).wait_recv()
            first(op[1], op[2])
        elif op[0] == "mix":
            mix(op[1])
        elif op[0] == "second":
            share(op[1], op[2], 1 - core).wait_recv()
            second(op[1], op[2])
        elif op[0] == "sum":
            sum_parts(op[1])
    for phase in (1, 2):
        finish(phase)
    for copy in sent:
        copy.wait_send()
    for phase in range(3):
        for source in SOURCES:
            share(phase, source, core).wait_send()
    for phase in (1, 2):
        z_copy(phase).wait_send()
        for k in range(8):
            copy, away = to_owner(phase, k)

            @pl.when(away)
            def _(copy=copy):
                copy.wait_send()


def applied_of(wavefunction, left_environment, combined, right_environment):
    ops, _ = schedule()
    vmem = pltpu.VMEM
    dma = pltpu.SemaphoreType.DMA
    count = len(MESSAGES)
    scratch = [
        vmem((1024, 3072), BF16), vmem((16, 192, 1536), BF16), vmem((16, 8, MAIN, 384), BF16),
        vmem((16, 8, REST, 384), BF16), vmem((1024, 1536), F32), vmem((512, 3072), BF16),
        vmem((512, 256), BF16), vmem((8, 512, 256), BF16), vmem((8, 512, 128), BF16),
        vmem((2, 3, 512, 256), BF16), vmem((2, 3, 512, 128), BF16),
        vmem((512, 256), F32), vmem((512, 128), F32), vmem((512, 256), BF16), vmem((512, 128), BF16),
        vmem((512, 256), BF16), vmem((512, 128), BF16),
        dma((4,)), dma((count,)), dma((count,)), dma((24,)), dma((24,)), dma((16,)), dma((12,)),
        dma((2,)), dma((2,)),
    ]
    spec = pl.BlockSpec(memory_space=pl.ANY)
    return pl.pallas_call(
        functools.partial(kernel, ops),
        out_shape=jax.ShapeDtypeStruct((4, 128, 384), BF16),
        in_specs=[spec, spec, spec, pl.BlockSpec(memory_space=pltpu.VMEM)],
        out_specs=pl.BlockSpec(memory_space=pltpu.VMEM),
        scratch_shapes=scratch,
        compiler_params=pltpu.CompilerParams(
            collective_id=0, has_side_effects=True, vmem_limit_bytes=61 << 20
        ),
    )(
        wavefunction.reshape(192, 1536),
        left_environment.reshape(1024, 3072),
        right_environment.transpose(0, 2, 1),
        combined,
    )


def combine_operators(operator_left, operator_right):
    channels = operator_left.shape[0]
    joined = jnp.einsum(
        "aups,uvqt->vpqast", operator_left, operator_right, precision=lax.Precision.HIGHEST
    )
    return joined.reshape(4 * channels, 4 * channels)


def split_up(value, dim, devices):
    before, after = (value.shape[:dim], value.shape[dim + 1 :])
    return jnp.moveaxis(value.reshape(*before, devices, -1, *after), dim, 0)


def sent_and_summed(value, axis, dim):
    parts = split_up(value, dim, lax.axis_size(axis))
    arrived = lax.all_to_all(parts, axis, split_axis=0, concat_axis=0, tiled=True)
    return arrived.astype(jnp.float32).sum(axis=0)


def shifted(value, axis, by):
    devices = lax.axis_size(axis)
    pairs = [(i, i + by) for i in range(devices) if 0 <= i + by < devices]
    return lax.ppermute(value, axis, pairs)


def label_at(labels, position):
    matches = jnp.arange(labels.shape[0], dtype=jnp.int32) == position
    return (jnp.sum(jnp.where(matches, labels, 0)), jnp.any(matches))


def tile_gram(left_tile, right_tile):
    return lax.dot_general(
        left_tile, right_tile, (((1,), (1,)), ((), ())), preferred_element_type=jnp.float32
    )


def shards(
    wavefunction, left_environment, operator_left, operator_right, right_environment, row_sector
):
    combined = combine_operators(operator_left, operator_right)
    raw = applied_of(wavefunction, left_environment, combined, right_environment)
    raw = raw.transpose(1, 0, 2)
    applied = jnp.concatenate(
        [raw[..., 0:128], raw[..., 256:320], raw[..., 128:256], raw[..., 320:384]], axis=2
    )
    row_count = 128
    own_tile = applied.reshape(row_count, 4 * 384)
    own_index = lax.axis_index(LB)
    tile_count = 16
    reach_tiles = SECTOR_TILES - 1
    own_label = label_at(row_sector, own_index)[0]
    buffer = jnp.zeros((row_count, (tile_count + 2 * reach_tiles) * row_count), jnp.float32)

    def place_block(buffer, gram_block, offset):
        mate_index = own_index + offset
        mate_label, inside = label_at(row_sector, mate_index)
        keep_block = jnp.logical_and(inside, mate_label == own_label)
        gram_block = jnp.where(keep_block, gram_block, jnp.float32(0.0))
        column_start = (mate_index + reach_tiles) * row_count
        return lax.dynamic_update_slice(buffer, gram_block, (jnp.int32(0), column_start))

    buffer = place_block(buffer, tile_gram(own_tile, own_tile), 0)
    for distance in range(1, SECTOR_TILES):
        gram_block = tile_gram(own_tile, shifted(own_tile, LB, -distance))
        buffer = place_block(buffer, gram_block, distance)
        returned = shifted(gram_block.astype(jnp.bfloat16), LB, distance).astype(gram_block.dtype)
        buffer = place_block(buffer, returned.T, -distance)
    full_rows = buffer[:, reach_tiles * row_count : (reach_tiles + tile_count) * row_count]
    density = sent_and_summed(full_rows.astype(jnp.bfloat16), RB, 1) * (
        1.0 / math.sqrt(4.0 * BOND_WIDTH)
    )
    return (applied, density)


def solution(mesh):
    torus = Mesh(mesh.devices.reshape(2, 4, 2, 4, 2), AXES)
    in_specs = (P(LB, None, RB), P(None, LB, None), P(), P(), P(None, RB, LB), P())
    out_specs = (P(LB, None, RB), P(LB, RB))
    return jax.shard_map(
        shards, mesh=torus, in_specs=in_specs, out_specs=out_specs, check_vma=False
    )
```

```python
import functools
import math

import jax
import jax.numpy as jnp
from jax import lax
from jax.experimental import pallas as pl
from jax.experimental.pallas import tpu as pltpu
from jax.sharding import Mesh
from jax.sharding import PartitionSpec as P

BOND_WIDTH = 3072
SECTOR_TILES = 4
AXES = ("zl", "y", "core", "x", "zh")
LB = ("zl", "y", "core")
RB = ("x", "zh")
BF16, F32 = jnp.bfloat16, jnp.float32

MAIN, REST = 128, 64
PIECES = (
    (("z", 1, 0, 64), ("z", -1, 64, 48), ("y", 1, 112, 32), ("y", -1, 144, 48)),
    (("z", 1, 0, 32), ("z", -1, 32, 32), ("y", 1, 64, 32), ("y", -1, 96, 32)),
    (("z", 1, 0, 32), ("z", -1, 32, 16), ("y", -1, 48, 16)),
)
UNIT_BYTES = (1536 * 2, 8 * 384 * 2, 8 * 384 * 2)
SHARD = (192, MAIN, REST)
SOURCES = tuple((dz, dy) for dz in (0, 1) for dy in range(4))
MESSAGES = tuple(
    (phase, piece, source)
    for phase in range(3)
    for piece in range(len(PIECES[phase]))
    for source in SOURCES[1:]
)


FIRSTS = (((0, 0),), ((0, 1), (0, 3)), ((1, 0),), ((1, 1), (1, 3)), ((0, 2), (1, 2)))
LATER = (("away", 10.0), ("keep", 1.0), ("finish", 6.0), ("swap", 0.5), ("gram", 9.0))


def forwards(phase, piece, source):
    tree, turn = PIECES[phase][piece][:2]
    (dz, dy), on, back = source, "+-"[turn < 0], (-turn) % 4
    named = lambda link, place: (link, (phase, piece, place))
    if tree == "z":
        if source == (1, 0):
            return [named("+", (1, 3)), named("-", (1, 1))]
        return [named(on, (dz, 2))] if dy == back else []
    if dz:
        return []
    across = [named("z", (1, dy))]
    return [named(on, (0, 2)), *across] if dy == back else across


def own_sends():
    for phase in range(3):
        pieces = range(len(PIECES[phase]))
        for piece in sorted(pieces, key=lambda p: PIECES[phase][p][0] == "y"):
            yield "z", (phase, piece, (1, 0))
        for piece in sorted(pieces, key=lambda p: PIECES[phase][p][0] == "z"):
            yield "+", (phase, piece, (0, 3))
            yield "-", (phase, piece, (0, 1))


def schedule(rate=43.5e3, lag=1.0, lead=5.0, step=0.05):
    spent = (None, 1.1, 0.7)
    waiting = {link: [] for link in "+-z"}
    for order, (link, message) in enumerate(own_sends()):
        waiting[link].append((message[0], order, message, True))
    free_at = dict.fromkeys("+-z", 0.0)
    arriving, beside, done, ops, issued = [], [], set(), [], []
    pieces_left = {(p, s): len(PIECES[p]) for p in range(3) for s in SOURCES[1:]}
    ready = {(p, s): None for p in range(3) for s in SOURCES}
    for phase in range(3):
        ready[phase, (0, 0)] = 4.0 + phase
    firsts, mixes, seconds = 0, 0, [0, 0]
    later = []
    order, now, tc_free = 1000, 0.0, 0.0
    while seconds[1] < 8:
        now += step
        for link in "+-z":
            if free_at[link] <= now and waiting[link]:
                job = min(waiting[link])
                waiting[link].remove(job)
                phase, piece, _ = message = job[2]
                took = PIECES[phase][piece][3] * UNIT_BYTES[phase] / rate
                if job[3]:
                    issued.append((max(0.0, now - lead), len(issued), link, message))
                free_at[link] = now + took
                arriving.append((now + took + lag, message))
        if tc_free > now:
            continue
        landed = [entry for entry in arriving if entry[0] <= now]
        if landed:
            entry = min(landed)
            arriving.remove(entry)
            message = entry[1]
            onward = forwards(*message)
            for link, passed in onward:
                order += 1
                waiting[link].append((passed[0], order, passed, False))
            ops.append((now, "take", message, onward))
            phase, _, source = message
            pieces_left[phase, source] -= 1
            if not pieces_left[phase, source]:
                ops.append((now, "share", phase, source))
                size = SHARD[phase] * UNIT_BYTES[phase]
                ready[phase, source] = now + 2.0 + size / 400e3
            tc_free = now + 0.2
            continue
        able = [k for k, at in ready.items() if at is not None and at <= now and k not in done]
        group = FIRSTS[firsts] if firsts < len(FIRSTS) else None
        due = [entry for entry in later if entry[0] <= now]
        if group is not None:
            if all((0, source) in able for source in group):
                done.update((0, source) for source in group)
                ops.append((now, "first", group, firsts == 0))
                firsts += 1
                tc_free = now + 1.0 + 1.1 * len(group)
        elif mixes < 4:
            ops.append((now, "mix", mixes))
            mixes += 1
            tc_free = now + 1.1
        elif due:
            later.remove(due[0])
            ops.append((now, *due[0][1:]))
            tc_free = now + 0.7
        elif able:
            phase, source = min(able, key=lambda k: (k[0], ready[k]))
            done.add((phase, source))
            ops.append((now, "second", phase, source))
            seconds[phase - 1] += 1
            tc_free = now + spent[phase]
            if phase == 1 and seconds[0] == 8:
                wait = 0.0
                for name, gap in LATER:
                    wait += gap
                    later.append((tc_free + wait, name, 1))
    ops += [(now, *entry[1:]) for entry in later]
    ops += [(now, name, 2) for name, _ in LATER]
    for at, _, link, message in reversed(issued):
        place = next((i for i, op in enumerate(ops) if op[0] > at), len(ops))
        ops.insert(place, (at, "send", link, message))
    return [op[1:] for op in ops], now


OFFSETS = (1, 2, 3, -1, -2, -3)


def row_device(m):
    return {"zl": m // 8, "y": lax.rem(m // 2, 4), "core": lax.rem(m, 2)}


def column_device(n):
    return {"x": n // 2, "zh": lax.rem(n, 2)}


def inside(m):
    return jnp.logical_and(m >= 0, m < 16)


def ring(value, by, size):
    return lax.rem(value + (by % size), size)


def kernel(
    ops, w_ref, l_ref, r_ref, comb_ref, sector_ref, out_ref, density_ref,
    left, wide, main, rest, acc, mixed, coef, part_main, part_rest, from_main, from_rest,
    kept_main, kept_rest, away_main, away_rest, back_main, back_rest,
    tile_main, tile_rest, mates_main, mates_rest, grams, turned, turned_out, turned_in, blocks_out, blocks_in,
    local_sem, send_sem, recv_sem, share_send, share_recv, x_send, x_recv, z_send, z_recv,
    swap_send, swap_recv, turn_send, turn_recv, block_send, block_recv,
):
    zl, y, core, x, zh = (lax.axis_index(a) for a in AXES)
    gathered = (wide, main, rest)
    number = {m: i for i, m in enumerate(MESSAGES)}
    neighbour = {
        "+": {"y": ring(y, 1, 4)},
        "-": {"y": ring(y, -1, 4)},
        "z": {"zl": 1 - zl},
    }
    mesh_type = pl.DeviceIdType.MESH

    def chip(source):
        dz, dy = source
        return (1 - zl if dz else zl) * 4 + ring(y, dy, 4)

    barrier = pltpu.get_barrier_semaphore()
    here = chip((0, 0)) * 2 + core
    column = x * 2 + zh
    partners = [*neighbour.values(), {"core": 1 - core}]
    partners += [column_device(ring(column, by, 8)) for by in range(1, 8)]
    for partner in partners:
        pl.semaphore_signal(barrier, inc=1, device_id=partner, device_id_type=mesh_type)
    mates = jnp.int32(0)
    for offset in OFFSETS:
        mates += inside(here + offset).astype(jnp.int32)

        @pl.when(inside(here + offset))
        def _(offset=offset):
            pl.semaphore_signal(
                barrier, inc=1, device_id=row_device(here + offset), device_id_type=mesh_type
            )

    loads = [
        pltpu.make_async_copy(w_ref, wide.at[here], local_sem.at[0]),
        pltpu.make_async_copy(r_ref.at[:, 0:MAIN], main.at[here], local_sem.at[1]),
        pltpu.make_async_copy(r_ref.at[:, MAIN : MAIN + REST], rest.at[here], local_sem.at[2]),
        pltpu.make_async_copy(l_ref, left, local_sem.at[3]),
    ]
    for load in loads:
        load.start()
    row = lax.broadcasted_iota(jnp.int32, (256, 32), 0)
    lane_at = lax.broadcasted_iota(jnp.int32, (256, 32), 1)
    spread = (row // 8 == lane_at).astype(BF16)
    row = lax.broadcasted_iota(jnp.int32, (256, 256), 0)
    lane_at = lax.broadcasted_iota(jnp.int32, (256, 256), 1)
    same = row % 8 == lane_at % 8
    high = comb_ref[...].astype(BF16)
    low = (comb_ref[...] - high.astype(F32)).astype(BF16)
    for at, term in enumerate((high, low)):
        tall = jnp.dot(spread, term, preferred_element_type=F32).astype(BF16)
        full = lax.dot_general(tall, spread, (((1,), (1,)), ((), ())), preferred_element_type=F32)
        coef[at * 256 : at * 256 + 256] = jnp.where(same, full, 0.0).astype(BF16)
    pl.semaphore_wait(barrier, len(partners) + mates)
    for load in loads:
        load.wait()

    sent = []

    def piece_of(message, receiver):
        phase, piece, _ = message
        start, size = PIECES[phase][piece][2:]
        if phase == 0:
            return wide.at[receiver, pl.ds(start, size)]
        return gathered[phase].at[receiver, :, pl.ds(start, size)]

    def send(link, message, source):
        block = piece_of(message, chip(source) * 2 + core)
        at = number[message]
        copy = pltpu.make_async_remote_copy(
            block, block, send_sem.at[at], recv_sem.at[at],
            device_id=neighbour[link], device_id_type=mesh_type,
        )
        copy.start()
        sent.append(copy)

    def arrived(message):
        block = piece_of(message, chip(message[2]) * 2 + core)
        at = number[message]
        pltpu.make_async_remote_copy(
            block, block, send_sem.at[at], recv_sem.at[at],
            device_id=neighbour["z"], device_id_type=mesh_type,
        ).wait_recv()

    def share(phase, source, owner):
        at = phase * 8 + SOURCES.index(source)
        block = gathered[phase].at[chip(source) * 2 + owner]
        return pltpu.make_async_remote_copy(
            block, block, share_send.at[at], share_recv.at[at],
            device_id={"core": 1 - core}, device_id_type=mesh_type,
        )

    def first(group, fresh):
        chips = [chip(source) for source in group]
        columns = [pl.ds(pl.multiple_of(k * 384, 384), 384) for k in chips]

        @pl.loop(0, 6)
        def _(tile):
            lanes = pl.ds(pl.multiple_of(tile * 256, 256), 256)
            block = [wide[pl.ds(k * 2, 2), :, lanes].reshape(384, 256) for k in chips]
            rows = [left[:, c] for c in columns]
            product = jnp.dot(
                jnp.concatenate(rows, axis=1), jnp.concatenate(block, axis=0),
                preferred_element_type=F32,
            )
            if fresh:
                acc[:, lanes] = product
            else:
                acc[:, lanes] += product

    def mix(quarter):
        @pl.loop(quarter * 2, quarter * 2 + 2)
        def _(group):
            halves = []
            for sub in range(2):
                start = pl.multiple_of(group * 16 + sub * 8, 8)
                stack = jnp.concatenate(
                    [
                        acc[pl.ds(a * 128 + start, 8), s * 384 : s * 384 + 384]
                        for a in range(8)
                        for s in range(4)
                    ],
                    axis=0,
                )
                top = stack.astype(BF16)
                under = (stack - top.astype(F32)).astype(BF16)
                both = jnp.dot(coef[...], top, preferred_element_type=F32)
                third = jnp.dot(coef[0:256], under, preferred_element_type=F32)
                halves.append(both[0:256] + both[256:512] + third)
            for v in range(8):
                for out_site in range(4):
                    at = (v * 4 + out_site) * 8
                    value = jnp.concatenate([h[at : at + 8] for h in halves], axis=0)
                    rows = pl.ds(pl.multiple_of(out_site * 128 + group * 16, 16), 16)
                    mixed[rows, v * 384 : v * 384 + 384] = value.astype(BF16)

    parts, froms = (None, part_main, part_rest), (None, from_main, from_rest)
    keeps, aways, backs = (None, kept_main, kept_rest), (None, away_main, away_rest), (None, back_main, back_rest)

    def to_owner(phase, k):
        owner, half = k // 2, lax.rem(k, 2)
        slot = lax.rem(x - owner + 7, 4)
        slot = jnp.minimum(slot, 2)
        copy = pltpu.make_async_remote_copy(
            parts[phase].at[k], froms[phase].at[half, slot],
            x_send.at[(phase - 1) * 8 + k], x_recv.at[(phase - 1) * 6 + half * 3 + slot],
            device_id={"x": owner}, device_id_type=mesh_type,
        )
        return copy, x != owner

    def second(phase, source):
        k = chip(source)
        width = 2 * SHARD[phase]

        total = None
        for v in range(0, 8, 2):
            block = [gathered[phase][pl.ds(k * 2, 2), v + j].reshape(width, 384) for j in (0, 1)]
            product = lax.dot_general(
                mixed[:, v * 384 : v * 384 + 768], jnp.concatenate(block, axis=1),
                (((1,), (1,)), ((), ())), preferred_element_type=F32,
            )
            total = product if total is None else total + product
        parts[phase][k] = total.astype(BF16)

        copy, away = to_owner(phase, k)

        @pl.when(away)
        def _():
            copy.start()

    def z_copy(phase):
        return pltpu.make_async_remote_copy(
            aways[phase], backs[phase], z_send.at[phase - 1], z_recv.at[phase - 1],
            device_id={"zh": 1 - zh}, device_id_type=mesh_type,
        )

    def sum_x(phase, half, put):
        for slot in range(3):
            pltpu.make_async_remote_copy(
                parts[phase].at[0], froms[phase].at[half, slot],
                x_send.at[0], x_recv.at[(phase - 1) * 6 + half * 3 + slot],
                device_id={"x": ring(x, 1, 4)}, device_id_type=mesh_type,
            ).wait_recv()

        @pl.loop(0, 8)
        def _(tile):
            rows = pl.ds(pl.multiple_of(tile * 64, 64), 64)
            total = parts[phase][x * 2 + half, rows].astype(F32)
            for slot in range(3):
                total += froms[phase][half, slot, rows].astype(F32)
            put(rows, total)

    def sum_away(phase):
        def put(rows, total):
            aways[phase][rows] = total.astype(BF16)

        sum_x(phase, 1 - zh, put)
        z_copy(phase).start()

    def sum_keep(phase):
        def put(rows, total):
            keeps[phase][rows] = total

        sum_x(phase, zh, put)

    tiles = (None, tile_main, tile_rest)
    mates_of = (None, mates_main, mates_rest)

    def finish(phase):
        z_copy(phase).wait_recv()
        for site in range(4):
            rows = slice(site * 128, site * 128 + 128)
            value = keeps[phase][rows] + backs[phase][rows].astype(F32)
            keeps[phase][rows] = value
            tiles[phase][site] = value.astype(BF16)

    def swap(phase, offset):
        half, at = int(offset > 0), abs(offset) - 1
        slot = ((phase - 1) * 2 + half) * 3 + at
        return pltpu.make_async_remote_copy(
            tiles[phase].at[pl.ds(half * 2, 2)], mates_of[phase].at[half, at],
            swap_send.at[slot], swap_recv.at[slot],
            device_id=row_device(here + offset), device_id_type=mesh_type,
        )

    def swaps(phase):
        for offset in OFFSETS:

            @pl.when(inside(here + offset))
            def _(offset=offset):
                swap(phase, offset).start()

    def nt(a, b):
        return lax.dot_general(a, b, (((1,), (1,)), ((), ())), preferred_element_type=F32)

    def gram(phase):
        width = 2 * SHARD[phase]
        for offset in OFFSETS:

            @pl.when(inside(here - offset))
            def _(offset=offset):
                swap(phase, offset).wait_recv()

        own = sum(nt(tiles[phase][site], tiles[phase][site]) for site in range(4))
        straight, crossed = [], []
        for half in (0, 1):
            mine = [tiles[phase][half * 2 + j] for j in (0, 1)]
            theirs = [mates_of[phase][half, :, j].reshape(384, width) for j in (0, 1)]
            straight.append(sum(nt(a, b) for a, b in zip(mine, theirs)))
            crossed.append(sum(nt(b, a) for a, b in zip(mine, theirs)))
        if phase == 1:
            grams[2, :, 0:128] = own
            for half in (0, 1):
                grams[half] = straight[half]
                turned[half] = crossed[half]
        else:
            grams[2, :, 0:128] += own
            for half in (0, 1):
                grams[half] += straight[half]
                turned_out[half] = (turned[half] + crossed[half]).astype(BF16)

    def turn(offset):
        half, at = int(offset < 0), abs(offset) - 1
        return pltpu.make_async_remote_copy(
            turned_out.at[half, pl.ds(at * 128, 128)], turned_in.at[1 - half, pl.ds(at * 128, 128)],
            turn_send.at[half * 3 + at], turn_recv.at[half * 3 + at],
            device_id=row_device(here + offset), device_id_type=mesh_type,
        )

    def block_copy(offset):
        mate = here + offset
        owner, half = mate // 2, lax.rem(mate, 2)
        return pltpu.make_async_remote_copy(
            blocks_out.at[offset + 3], blocks_in.at[half, column],
            block_send.at[offset + 3], block_recv.at[half * 8 + column],
            device_id=column_device(owner), device_id_type=mesh_type,
        )

    def reach():
        for offset in OFFSETS:

            @pl.when(inside(here + offset))
            def _(offset=offset):
                turn(offset).start()

        for offset in (0, *OFFSETS):
            half, at = int(offset < 0), abs(offset) - 1

            @pl.when(inside(here + offset))
            def _(offset=offset, half=half, at=at):
                if offset:
                    turn(-offset).wait_recv()
                    came = turned_in[half, at * 128 : at * 128 + 128].astype(F32)
                    value = grams[half, :, at * 128 : at * 128 + 128] + came
                else:
                    value = grams[2, :, 0:128]
                owner = (here + offset) // 2

                @pl.when(owner == column)
                def _():
                    blocks_in[lax.rem(here + offset, 2), column] = value.astype(BF16)

                @pl.when(owner != column)
                def _():
                    blocks_out[offset + 3] = value.astype(BF16)
                    block_copy(offset).start()

        for half in (0, 1):
            mate = column * 2 + half
            near = jnp.logical_and(mate - here <= 3, here - mate <= 3)
            lanes = slice(half * 128, half * 128 + 128)

            @pl.when(near)
            def _(half=half, mate=mate, lanes=lanes):
                for by in range(1, 8):
                    source = ring(column, by, 8)
                    pltpu.make_async_remote_copy(
                        blocks_out.at[0], blocks_in.at[half, source],
                        block_send.at[0], block_recv.at[half * 8 + source],
                        device_id=column_device(source), device_id_type=mesh_type,
                    ).wait_recv()
                total = sum(blocks_in[half, n].astype(F32) for n in range(8))
                same_sector = sector_ref[mate] == sector_ref[here]
                total = total * (1.0 / math.sqrt(4.0 * BOND_WIDTH))
                density_ref[:, lanes] = jnp.where(same_sector, total, 0.0)

            @pl.when(jnp.logical_not(near))
            def _(lanes=lanes):
                density_ref[:, lanes] = jnp.zeros((128, 128), F32)

    def write_out():
        lane = lax.broadcasted_iota(jnp.int32, (128, 128), 1)
        for site in range(4):
            rows = slice(site * 128, site * 128 + 128)
            out_ref[site, :, 0:128] = tile_main[site, :, 0:128]
            rolled = pltpu.roll(kept_main[rows, 128:256], 64, 1)
            last = kept_rest[rows, :]
            out_ref[site, :, 128:256] = jnp.where(lane < 64, last, rolled).astype(BF16)
            out_ref[site, :, 256:384] = jnp.where(lane < 64, rolled, last).astype(BF16)

    after = dict(away=sum_away, keep=sum_keep, finish=finish, swap=swaps, gram=gram)
    for phase in range(3):
        share(phase, (0, 0), core).start()
    for op in ops:
        if op[0] == "send":
            send(op[1], op[2], (0, 0))
        elif op[0] == "take":
            arrived(op[1])
            for link, passed in op[2]:
                send(link, passed, op[1][2])
        elif op[0] == "share":
            share(op[1], op[2], core).start()
        elif op[0] == "first":
            for source in op[1]:
                share(0, source, 1 - core).wait_recv()
            first(op[1], op[2])
        elif op[0] == "mix":
            mix(op[1])
        elif op[0] == "second":
            share(op[1], op[2], 1 - core).wait_recv()
            second(op[1], op[2])
        else:
            if op == ("gram", 2):
                write_out()
            after[op[0]](op[1])
    reach()
    for copy in sent:
        copy.wait_send()
    for phase in range(3):
        for source in SOURCES:
            share(phase, source, core).wait_send()
    for phase in (1, 2):
        z_copy(phase).wait_send()
        for k in range(8):
            copy, away = to_owner(phase, k)

            @pl.when(away)
            def _(copy=copy):
                copy.wait_send()

    for offset in OFFSETS:

        @pl.when(inside(here + offset))
        def _(offset=offset):
            swap(1, offset).wait_send()
            swap(2, offset).wait_send()
            turn(offset).wait_send()

    for offset in (0, *OFFSETS):

        @pl.when(jnp.logical_and(inside(here + offset), (here + offset) // 2 != column))
        def _(offset=offset):
            block_copy(offset).wait_send()


def fused(wavefunction, left_environment, combined, right_environment, row_sector):
    ops, _ = schedule()
    vmem = pltpu.VMEM
    dma = pltpu.SemaphoreType.DMA
    count = len(MESSAGES)
    scratch = [
        vmem((1024, 3072), BF16), vmem((16, 192, 1536), BF16), vmem((16, 8, MAIN, 384), BF16),
        vmem((16, 8, REST, 384), BF16), vmem((1024, 1536), F32), vmem((512, 3072), BF16),
        vmem((512, 256), BF16), vmem((8, 512, 256), BF16), vmem((8, 512, 128), BF16),
        vmem((2, 3, 512, 256), BF16), vmem((2, 3, 512, 128), BF16),
        vmem((512, 256), F32), vmem((512, 128), F32), vmem((512, 256), BF16), vmem((512, 128), BF16),
        vmem((512, 256), BF16), vmem((512, 128), BF16),
        vmem((4, 128, 256), BF16), vmem((4, 128, 128), BF16), vmem((2, 3, 2, 128, 256), BF16),
        vmem((2, 3, 2, 128, 128), BF16), vmem((3, 128, 384), F32), vmem((2, 384, 128), F32),
        vmem((2, 384, 128), BF16), vmem((2, 384, 128), BF16), vmem((7, 128, 128), BF16),
        vmem((2, 8, 128, 128), BF16),
        dma((4,)), dma((count,)), dma((count,)), dma((24,)), dma((24,)), dma((16,)), dma((12,)),
        dma((2,)), dma((2,)), dma((12,)), dma((12,)), dma((6,)), dma((6,)), dma((7,)), dma((16,)),
    ]
    spec = pl.BlockSpec(memory_space=pl.ANY)
    return pl.pallas_call(
        functools.partial(kernel, ops),
        out_shape=(
            jax.ShapeDtypeStruct((4, 128, 384), BF16), jax.ShapeDtypeStruct((128, 256), F32)
        ),
        in_specs=[spec, spec, spec, pl.BlockSpec(memory_space=pltpu.VMEM),
                  pl.BlockSpec(memory_space=pltpu.SMEM)],
        out_specs=(pl.BlockSpec(memory_space=pltpu.VMEM),) * 2,
        scratch_shapes=scratch,
        compiler_params=pltpu.CompilerParams(
            collective_id=0, has_side_effects=True, vmem_limit_bytes=61 << 20
        ),
    )(
        wavefunction.reshape(192, 1536),
        left_environment.reshape(1024, 3072),
        right_environment.transpose(0, 2, 1),
        combined,
        row_sector,
    )


def combine_operators(operator_left, operator_right):
    channels = operator_left.shape[0]
    joined = jnp.einsum(
        "aups,uvqt->vpqast", operator_left, operator_right, precision=lax.Precision.HIGHEST
    )
    return joined.reshape(4 * channels, 4 * channels)


def shards(
    wavefunction, left_environment, operator_left, operator_right, right_environment, row_sector
):
    combined = combine_operators(operator_left, operator_right)
    raw, density = fused(
        wavefunction, left_environment, combined, right_environment, row_sector
    )
    return raw.transpose(1, 0, 2), density


def solution(mesh):
    torus = Mesh(mesh.devices.reshape(2, 4, 2, 4, 2), AXES)
    in_specs = (P(LB, None, RB), P(None, LB, None), P(), P(), P(None, RB, LB), P())
    out_specs = (P(LB, None, RB), P(LB, RB))
    return jax.shard_map(
        shards, mesh=torus, in_specs=in_specs, out_specs=out_specs, check_vma=False
    )
```

```python
import functools
import math

import jax
import jax.numpy as jnp
from jax import lax
from jax.experimental import pallas as pl
from jax.experimental.pallas import tpu as pltpu
from jax.sharding import Mesh
from jax.sharding import PartitionSpec as P

BOND_WIDTH = 3072
SECTOR_TILES = 4
AXES = ("zl", "y", "core", "x", "zh")
LB = ("zl", "y", "core")
RB = ("x", "zh")
BF16, F32 = jnp.bfloat16, jnp.float32

MAIN, REST = 128, 64
PIECES = (
    (("z", 1, 0, 64), ("z", -1, 64, 48), ("y", 1, 112, 32), ("y", -1, 144, 48)),
    (("z", 1, 0, 32), ("z", -1, 32, 32), ("y", 1, 64, 32), ("y", -1, 96, 32)),
    (("z", 1, 0, 16), ("z", -1, 16, 16), ("y", 1, 32, 16), ("y", -1, 48, 16)),
)
UNIT_BYTES = (1536 * 2, 8 * 384 * 2, 8 * 384 * 2)
SHARD = (192, MAIN, REST)
SOURCES = tuple((dz, dy) for dz in (0, 1) for dy in range(4))
MESSAGES = tuple(
    (phase, piece, source)
    for phase in range(3)
    for piece in range(len(PIECES[phase]))
    for source in SOURCES[1:]
)


FIRSTS = (((0, 0),), ((0, 1), (0, 3)), ((1, 0),), ((1, 1), (1, 3)), ((0, 2), (1, 2)))
LATER = (("away", 10.0), ("keep", 1.0), ("finish", 6.0), ("swap", 0.5), ("gram", 9.0))


def forwards(phase, piece, source):
    tree, turn = PIECES[phase][piece][:2]
    (dz, dy), on, back = source, "+-"[turn < 0], (-turn) % 4
    named = lambda link, place: (link, (phase, piece, place))
    if tree == "z":
        if source == (1, 0):
            return [named("+", (1, 3)), named("-", (1, 1))]
        return [named(on, (dz, 2))] if dy == back else []
    if dz:
        return []
    across = [named("z", (1, dy))]
    return [named(on, (0, 2)), *across] if dy == back else across


def own_sends():
    for phase in range(3):
        pieces = range(len(PIECES[phase]))
        for piece in sorted(pieces, key=lambda p: PIECES[phase][p][0] == "y"):
            yield "z", (phase, piece, (1, 0))
        for piece in sorted(pieces, key=lambda p: PIECES[phase][p][0] == "z"):
            yield "+", (phase, piece, (0, 3))
            yield "-", (phase, piece, (0, 1))


def schedule(rate=43.5e3, lag=1.0, lead=5.0, step=0.05):
    spent = (None, 1.1, 0.7)
    waiting = {link: [] for link in "+-z"}
    for order, (link, message) in enumerate(own_sends()):
        waiting[link].append((message[0], order, message, True))
    free_at = dict.fromkeys("+-z", 0.0)
    arriving, beside, done, ops, issued = [], [], set(), [], []
    pieces_left = {(p, s): len(PIECES[p]) for p in range(3) for s in SOURCES[1:]}
    ready = {(p, s): None for p in range(3) for s in SOURCES}
    for phase in range(3):
        ready[phase, (0, 0)] = 4.0 + phase
    firsts, mixes, seconds = 0, 0, [0, 0]
    later = []
    order, now, tc_free = 1000, 0.0, 0.0
    while seconds[1] < 8:
        now += step
        for link in "+-z":
            if free_at[link] <= now and waiting[link]:
                job = min(waiting[link])
                waiting[link].remove(job)
                phase, piece, _ = message = job[2]
                took = PIECES[phase][piece][3] * UNIT_BYTES[phase] / rate
                if job[3]:
                    issued.append((max(0.0, now - lead), len(issued), link, message))
                free_at[link] = now + took
                arriving.append((now + took + lag, message))
        if tc_free > now:
            continue
        landed = [entry for entry in arriving if entry[0] <= now]
        if landed:
            entry = min(landed)
            arriving.remove(entry)
            message = entry[1]
            onward = forwards(*message)
            for link, passed in onward:
                order += 1
                waiting[link].append((passed[0], order, passed, False))
            ops.append((now, "take", message, onward))
            phase, _, source = message
            pieces_left[phase, source] -= 1
            if not pieces_left[phase, source]:
                ops.append((now, "share", phase, source))
                size = SHARD[phase] * UNIT_BYTES[phase]
                ready[phase, source] = now + 2.0 + size / 400e3
            tc_free = now + 0.2
            continue
        able = [k for k, at in ready.items() if at is not None and at <= now and k not in done]
        group = FIRSTS[firsts] if firsts < len(FIRSTS) else None
        due = [entry for entry in later if entry[0] <= now]
        if due and due[0][1] == "first":
            later.remove(due[0])
            ops.append((now, *due[0][1:]))
            tc_free = now + 0.4 + 0.6 * len(due[0][2])
        elif group is not None:
            if all((0, source) in able for source in group):
                done.update((0, source) for source in group)
                for part in (0, 1):
                    later.append((now, "first", group, firsts == 0, part))
                firsts += 1
        elif mixes < 4:
            ops.append((now, "mix", mixes))
            mixes += 1
            tc_free = now + 1.1
        elif due:
            later.remove(due[0])
            ops.append((now, *due[0][1:]))
            tc_free = now + 0.7
        elif able:
            phase, source = min(able, key=lambda k: (k[0], ready[k]))
            done.add((phase, source))
            ops.append((now, "second", phase, source))
            seconds[phase - 1] += 1
            tc_free = now + spent[phase]
            if phase == 1 and seconds[0] == 8:
                wait = 0.0
                for name, gap in LATER:
                    wait += gap
                    later.append((tc_free + wait, name, 1))
    ops += [(now, *entry[1:]) for entry in later]
    ops += [(now, name, 2) for name, _ in LATER]
    for at, _, link, message in reversed(issued):
        place = next((i for i, op in enumerate(ops) if op[0] > at), len(ops))
        ops.insert(place, (at, "send", link, message))
    return [op[1:] for op in ops], now


OFFSETS = (1, 2, 3, -1, -2, -3)


def row_device(m):
    return {"zl": m // 8, "y": lax.rem(m // 2, 4), "core": lax.rem(m, 2)}


def column_device(n):
    return {"x": n // 2, "zh": lax.rem(n, 2)}


def inside(m):
    return jnp.logical_and(m >= 0, m < 16)


def ring(value, by, size):
    return lax.rem(value + (by % size), size)


def kernel(
    ops, w_ref, l_ref, r_ref, ol_ref, or_ref, sector_ref, out_ref, density_ref,
    left, wide, main, rest, acc, mixed, coef, part_main, part_rest, from_main, from_rest,
    kept_main, kept_rest, away_main, away_rest, back_main, back_rest,
    tile_main, tile_rest, mates_main, mates_rest, grams, turned, turned_out, turned_in, blocks_out, blocks_in,
    local_sem, send_sem, recv_sem, share_send, share_recv, x_send, x_recv, z_send, z_recv,
    swap_send, swap_recv, turn_send, turn_recv, block_send, block_recv,
):
    zl, y, core, x, zh = (lax.axis_index(a) for a in AXES)
    gathered = (wide, main, rest)
    number = {m: i for i, m in enumerate(MESSAGES)}
    neighbour = {
        "+": {"y": ring(y, 1, 4)},
        "-": {"y": ring(y, -1, 4)},
        "z": {"zl": 1 - zl},
    }
    mesh_type = pl.DeviceIdType.MESH

    def chip(source):
        dz, dy = source
        return (1 - zl if dz else zl) * 4 + ring(y, dy, 4)

    barrier = pltpu.get_barrier_semaphore()
    here = chip((0, 0)) * 2 + core
    column = x * 2 + zh
    partners = [*neighbour.values(), {"core": 1 - core}]
    partners += [column_device(ring(column, by, 8)) for by in range(1, 8)]
    for partner in partners:
        pl.semaphore_signal(barrier, inc=1, device_id=partner, device_id_type=mesh_type)
    mates = jnp.int32(0)
    for offset in OFFSETS:
        mates += inside(here + offset).astype(jnp.int32)

        @pl.when(inside(here + offset))
        def _(offset=offset):
            pl.semaphore_signal(
                barrier, inc=1, device_id=row_device(here + offset), device_id_type=mesh_type
            )

    loads = [
        pltpu.make_async_copy(w_ref, wide.at[here], local_sem.at[0]),
        pltpu.make_async_copy(r_ref.at[:, 0:MAIN], main.at[here], local_sem.at[1]),
        pltpu.make_async_copy(r_ref.at[:, MAIN : MAIN + REST], rest.at[here], local_sem.at[2]),
        pltpu.make_async_copy(l_ref, left, local_sem.at[3]),
    ]
    for load in loads:
        load.start()
    pl.semaphore_wait(barrier, len(partners) + mates)
    for load in loads[:3]:
        load.wait()

    sent = []

    def piece_of(message, receiver):
        phase, piece, _ = message
        start, size = PIECES[phase][piece][2:]
        if phase == 0:
            return wide.at[receiver, pl.ds(start, size)]
        return gathered[phase].at[receiver, :, pl.ds(start, size)]

    def send(link, message, source):
        block = piece_of(message, chip(source) * 2 + core)
        at = number[message]
        copy = pltpu.make_async_remote_copy(
            block, block, send_sem.at[at], recv_sem.at[at],
            device_id=neighbour[link], device_id_type=mesh_type,
        )
        copy.start()
        sent.append(copy)

    def arrived(message):
        block = piece_of(message, chip(message[2]) * 2 + core)
        at = number[message]
        pltpu.make_async_remote_copy(
            block, block, send_sem.at[at], recv_sem.at[at],
            device_id=neighbour["z"], device_id_type=mesh_type,
        ).wait_recv()

    def share(phase, source, owner):
        at = phase * 8 + SOURCES.index(source)
        block = gathered[phase].at[chip(source) * 2 + owner]
        return pltpu.make_async_remote_copy(
            block, block, share_send.at[at], share_recv.at[at],
            device_id={"core": 1 - core}, device_id_type=mesh_type,
        )

    def coefficients():
        def of(size, dim):
            return lax.broadcasted_iota(jnp.int32, size, dim)

        def dot(a, b, dims=(((1,), (0,)), ((), ()))):
            return lax.dot_general(
                a, b, dims, precision=lax.Precision.HIGHEST, preferred_element_type=F32
            )

        across = (((1,), (1,)), ((), ()))
        tall, short = of((256, 32), 0), of((256, 32), 1)
        pick = (of((256, 8), 0) // 32 == of((256, 8), 1)).astype(F32)
        right = dot(pick, or_ref[...].reshape(32, 8), across)
        right = jnp.where(tall // 8 % 2 == short // 2 % 2, right, 0.0)
        i, j = of((32, 32), 0), of((32, 32), 1)
        right = dot(right, jnp.logical_and(i // 4 == j // 4, i % 2 == j % 2).astype(F32))
        right = jnp.where(tall // 16 % 2 == short // 2 % 2, right, 0.0)
        lefts = ol_ref[...].reshape(32, 8)
        total = None
        for site in (0, 1):
            wanted = jnp.logical_and(tall // 32 == short // 4, tall // 16 % 2 == short % 2)
            wanted = jnp.logical_and(wanted, short // 2 % 2 == site).astype(F32)
            i, j = of((8, 32), 0), of((8, 32), 1)
            place = jnp.logical_and(i == j // 4, j // 2 % 2 == site).astype(F32)
            term = dot(dot(wanted, lefts), place)
            total = term if total is None else total + term
        total = jnp.where(tall // 8 % 2 == short % 2, total, 0.0)
        full = dot(right, total, across)
        full = jnp.where(of((256, 256), 0) % 8 == of((256, 256), 1) % 8, full, 0.0)
        high = full.astype(BF16)
        coef[0:256] = high
        coef[256:512] = (full - high.astype(F32)).astype(BF16)

    def first(group, fresh, part):
        chips = [chip(source) for source in group]
        columns = [pl.ds(pl.multiple_of(k * 384, 384), 384) for k in chips]

        @pl.loop(part * 3, part * 3 + 3)
        def _(tile):
            lanes = pl.ds(pl.multiple_of(tile * 256, 256), 256)
            block = [wide[pl.ds(k * 2, 2), :, lanes].reshape(384, 256) for k in chips]
            rows = [left[:, c] for c in columns]
            product = jnp.dot(
                jnp.concatenate(rows, axis=1), jnp.concatenate(block, axis=0),
                preferred_element_type=F32,
            )
            if fresh:
                acc[:, lanes] = product
            else:
                acc[:, lanes] += product

    def mix(quarter):
        @pl.loop(quarter * 2, quarter * 2 + 2)
        def _(group):
            halves = []
            for sub in range(2):
                start = pl.multiple_of(group * 16 + sub * 8, 8)
                stack = jnp.concatenate(
                    [
                        acc[pl.ds(a * 128 + start, 8), s * 384 : s * 384 + 384]
                        for a in range(8)
                        for s in range(4)
                    ],
                    axis=0,
                )
                top = stack.astype(BF16)
                under = (stack - top.astype(F32)).astype(BF16)
                both = jnp.dot(coef[...], top, preferred_element_type=F32)
                third = jnp.dot(coef[0:256], under, preferred_element_type=F32)
                halves.append(both[0:256] + both[256:512] + third)
            for v in range(8):
                for out_site in range(4):
                    at = (v * 4 + out_site) * 8
                    value = jnp.concatenate([h[at : at + 8] for h in halves], axis=0)
                    rows = pl.ds(pl.multiple_of(out_site * 128 + group * 16, 16), 16)
                    mixed[rows, v * 384 : v * 384 + 384] = value.astype(BF16)

    parts, froms = (None, part_main, part_rest), (None, from_main, from_rest)
    keeps, aways, backs = (None, kept_main, kept_rest), (None, away_main, away_rest), (None, back_main, back_rest)

    def to_owner(phase, k):
        owner, half = k // 2, lax.rem(k, 2)
        slot = lax.rem(x - owner + 7, 4)
        slot = jnp.minimum(slot, 2)
        copy = pltpu.make_async_remote_copy(
            parts[phase].at[k], froms[phase].at[half, slot],
            x_send.at[(phase - 1) * 8 + k], x_recv.at[(phase - 1) * 6 + half * 3 + slot],
            device_id={"x": owner}, device_id_type=mesh_type,
        )
        return copy, x != owner

    def second(phase, source):
        k = chip(source)
        width = 2 * SHARD[phase]

        total = None
        for v in range(0, 8, 2):
            block = [gathered[phase][pl.ds(k * 2, 2), v + j].reshape(width, 384) for j in (0, 1)]
            product = lax.dot_general(
                mixed[:, v * 384 : v * 384 + 768], jnp.concatenate(block, axis=1),
                (((1,), (1,)), ((), ())), preferred_element_type=F32,
            )
            total = product if total is None else total + product
        parts[phase][k] = total.astype(BF16)

        copy, away = to_owner(phase, k)

        @pl.when(away)
        def _():
            copy.start()

    def z_copy(phase):
        return pltpu.make_async_remote_copy(
            aways[phase], backs[phase], z_send.at[phase - 1], z_recv.at[phase - 1],
            device_id={"zh": 1 - zh}, device_id_type=mesh_type,
        )

    def sum_x(phase, half, put):
        for slot in range(3):
            pltpu.make_async_remote_copy(
                parts[phase].at[0], froms[phase].at[half, slot],
                x_send.at[0], x_recv.at[(phase - 1) * 6 + half * 3 + slot],
                device_id={"x": ring(x, 1, 4)}, device_id_type=mesh_type,
            ).wait_recv()

        @pl.loop(0, 8)
        def _(tile):
            rows = pl.ds(pl.multiple_of(tile * 64, 64), 64)
            total = parts[phase][x * 2 + half, rows].astype(F32)
            for slot in range(3):
                total += froms[phase][half, slot, rows].astype(F32)
            put(rows, total)

    def sum_away(phase):
        def put(rows, total):
            aways[phase][rows] = total.astype(BF16)

        sum_x(phase, 1 - zh, put)
        z_copy(phase).start()

    def sum_keep(phase):
        def put(rows, total):
            keeps[phase][rows] = total

        sum_x(phase, zh, put)

    tiles = (None, tile_main, tile_rest)
    mates_of = (None, mates_main, mates_rest)

    def finish(phase):
        z_copy(phase).wait_recv()
        for site in range(4):
            rows = slice(site * 128, site * 128 + 128)
            value = keeps[phase][rows] + backs[phase][rows].astype(F32)
            keeps[phase][rows] = value
            tiles[phase][site] = value.astype(BF16)

    def swap(phase, offset):
        half, at = int(offset > 0), abs(offset) - 1
        slot = ((phase - 1) * 2 + half) * 3 + at
        return pltpu.make_async_remote_copy(
            tiles[phase].at[pl.ds(half * 2, 2)], mates_of[phase].at[half, at],
            swap_send.at[slot], swap_recv.at[slot],
            device_id=row_device(here + offset), device_id_type=mesh_type,
        )

    def swaps(phase):
        for offset in OFFSETS:

            @pl.when(inside(here + offset))
            def _(offset=offset):
                swap(phase, offset).start()

    def nt(a, b):
        return lax.dot_general(a, b, (((1,), (1,)), ((), ())), preferred_element_type=F32)

    def gram(phase):
        width = 2 * SHARD[phase]
        for offset in OFFSETS:

            @pl.when(inside(here - offset))
            def _(offset=offset):
                swap(phase, offset).wait_recv()

        own = sum(nt(tiles[phase][site], tiles[phase][site]) for site in range(4))
        straight, crossed = [], []
        for half in (0, 1):
            mine = [tiles[phase][half * 2 + j] for j in (0, 1)]
            theirs = [mates_of[phase][half, :, j].reshape(384, width) for j in (0, 1)]
            straight.append(sum(nt(a, b) for a, b in zip(mine, theirs)))
            crossed.append(sum(nt(b, a) for a, b in zip(mine, theirs)))
        if phase == 1:
            grams[2, :, 0:128] = own
            for half in (0, 1):
                grams[half] = straight[half]
                turned[half] = crossed[half]
        else:
            grams[2, :, 0:128] += own
            for half in (0, 1):
                grams[half] += straight[half]
                turned_out[half] = (turned[half] + crossed[half]).astype(BF16)

    def turn(offset):
        half, at = int(offset < 0), abs(offset) - 1
        return pltpu.make_async_remote_copy(
            turned_out.at[half, pl.ds(at * 128, 128)], turned_in.at[1 - half, pl.ds(at * 128, 128)],
            turn_send.at[half * 3 + at], turn_recv.at[half * 3 + at],
            device_id=row_device(here + offset), device_id_type=mesh_type,
        )

    def block_copy(offset):
        mate = here + offset
        owner, half = mate // 2, lax.rem(mate, 2)
        return pltpu.make_async_remote_copy(
            blocks_out.at[offset + 3], blocks_in.at[half, column],
            block_send.at[offset + 3], block_recv.at[half * 8 + column],
            device_id=column_device(owner), device_id_type=mesh_type,
        )

    def reach():
        for offset in OFFSETS:

            @pl.when(inside(here + offset))
            def _(offset=offset):
                turn(offset).start()

        for offset in (0, *OFFSETS):
            half, at = int(offset < 0), abs(offset) - 1

            @pl.when(inside(here + offset))
            def _(offset=offset, half=half, at=at):
                if offset:
                    turn(-offset).wait_recv()
                    came = turned_in[half, at * 128 : at * 128 + 128].astype(F32)
                    value = grams[half, :, at * 128 : at * 128 + 128] + came
                else:
                    value = grams[2, :, 0:128]
                owner = (here + offset) // 2

                @pl.when(owner == column)
                def _():
                    blocks_in[lax.rem(here + offset, 2), column] = value.astype(BF16)

                @pl.when(owner != column)
                def _():
                    blocks_out[offset + 3] = value.astype(BF16)
                    block_copy(offset).start()

        for half in (0, 1):
            mate = column * 2 + half
            near = jnp.logical_and(mate - here <= 3, here - mate <= 3)
            lanes = slice(half * 128, half * 128 + 128)

            @pl.when(near)
            def _(half=half, mate=mate, lanes=lanes):
                for by in range(1, 8):
                    source = ring(column, by, 8)
                    pltpu.make_async_remote_copy(
                        blocks_out.at[0], blocks_in.at[half, source],
                        block_send.at[0], block_recv.at[half * 8 + source],
                        device_id=column_device(source), device_id_type=mesh_type,
                    ).wait_recv()
                total = sum(blocks_in[half, n].astype(F32) for n in range(8))
                same_sector = sector_ref[mate] == sector_ref[here]
                total = total * (1.0 / math.sqrt(4.0 * BOND_WIDTH))
                density_ref[:, lanes] = jnp.where(same_sector, total, 0.0)

            @pl.when(jnp.logical_not(near))
            def _(lanes=lanes):
                density_ref[:, lanes] = jnp.zeros((128, 128), F32)

    def write_out():
        lane = lax.broadcasted_iota(jnp.int32, (128, 128), 1)
        for site in range(4):
            rows = slice(site * 128, site * 128 + 128)
            out_ref[site, :, 0:128] = tile_main[site, :, 0:128]
            rolled = pltpu.roll(kept_main[rows, 128:256], 64, 1)
            last = kept_rest[rows, :]
            out_ref[site, :, 128:256] = jnp.where(lane < 64, last, rolled).astype(BF16)
            out_ref[site, :, 256:384] = jnp.where(lane < 64, rolled, last).astype(BF16)

    after = dict(away=sum_away, keep=sum_keep, finish=finish, swap=swaps, gram=gram)
    for phase in range(3):
        share(phase, (0, 0), core).start()
    for op in ops:
        if op[0] == "first" and op[2] and not op[3]:
            coefficients()
        if op[0] == "send":
            send(op[1], op[2], (0, 0))
        elif op[0] == "take":
            arrived(op[1])
            for link, passed in op[2]:
                send(link, passed, op[1][2])
        elif op[0] == "share":
            share(op[1], op[2], core).start()
        elif op[0] == "first":
            if not op[3]:
                for source in op[1]:
                    share(0, source, 1 - core).wait_recv()
            if op[2] and not op[3]:
                loads[3].wait()
            first(*op[1:])
        elif op[0] == "mix":
            mix(op[1])
        elif op[0] == "second":
            share(op[1], op[2], 1 - core).wait_recv()
            second(op[1], op[2])
        else:
            if op == ("gram", 2):
                write_out()
            after[op[0]](op[1])
    reach()
    for copy in sent:
        copy.wait_send()
    for phase in range(3):
        for source in SOURCES:
            share(phase, source, core).wait_send()
    for phase in (1, 2):
        z_copy(phase).wait_send()
        for k in range(8):
            copy, away = to_owner(phase, k)

            @pl.when(away)
            def _(copy=copy):
                copy.wait_send()

    for offset in OFFSETS:

        @pl.when(inside(here + offset))
        def _(offset=offset):
            swap(1, offset).wait_send()
            swap(2, offset).wait_send()
            turn(offset).wait_send()

    for offset in (0, *OFFSETS):

        @pl.when(jnp.logical_and(inside(here + offset), (here + offset) // 2 != column))
        def _(offset=offset):
            block_copy(offset).wait_send()


def fused(wavefunction, left_environment, operator_left, operator_right, right_environment, row_sector):
    ops, _ = schedule()
    vmem = pltpu.VMEM
    dma = pltpu.SemaphoreType.DMA
    count = len(MESSAGES)
    scratch = [
        vmem((1024, 3072), BF16), vmem((16, 192, 1536), BF16), vmem((16, 8, MAIN, 384), BF16),
        vmem((16, 8, REST, 384), BF16), vmem((1024, 1536), F32), vmem((512, 3072), BF16),
        vmem((512, 256), BF16), vmem((8, 512, 256), BF16), vmem((8, 512, 128), BF16),
        vmem((2, 3, 512, 256), BF16), vmem((2, 3, 512, 128), BF16),
        vmem((512, 256), F32), vmem((512, 128), F32), vmem((512, 256), BF16), vmem((512, 128), BF16),
        vmem((512, 256), BF16), vmem((512, 128), BF16),
        vmem((4, 128, 256), BF16), vmem((4, 128, 128), BF16), vmem((2, 3, 2, 128, 256), BF16),
        vmem((2, 3, 2, 128, 128), BF16), vmem((3, 128, 384), F32), vmem((2, 384, 128), F32),
        vmem((2, 384, 128), BF16), vmem((2, 384, 128), BF16), vmem((7, 128, 128), BF16),
        vmem((2, 8, 128, 128), BF16),
        dma((4,)), dma((count,)), dma((count,)), dma((24,)), dma((24,)), dma((16,)), dma((12,)),
        dma((2,)), dma((2,)), dma((12,)), dma((12,)), dma((6,)), dma((6,)), dma((7,)), dma((16,)),
    ]
    spec = pl.BlockSpec(memory_space=pl.ANY)
    return pl.pallas_call(
        functools.partial(kernel, ops),
        out_shape=(
            jax.ShapeDtypeStruct((4, 128, 384), BF16), jax.ShapeDtypeStruct((128, 256), F32)
        ),
        in_specs=[spec] * 3 + [pl.BlockSpec(memory_space=pltpu.VMEM)] * 2
        + [pl.BlockSpec(memory_space=pltpu.SMEM)],
        out_specs=(pl.BlockSpec(memory_space=pltpu.VMEM),) * 2,
        scratch_shapes=scratch,
        compiler_params=pltpu.CompilerParams(
            collective_id=0, has_side_effects=True, vmem_limit_bytes=61 << 20
        ),
    )(
        wavefunction.reshape(192, 1536),
        left_environment.reshape(1024, 3072),
        right_environment.transpose(0, 2, 1),
        operator_left.transpose(0, 2, 3, 1),
        operator_right.transpose(0, 2, 3, 1),
        row_sector,
    )


def shards(
    wavefunction, left_environment, operator_left, operator_right, right_environment, row_sector
):
    raw, density = fused(
        wavefunction, left_environment, operator_left, operator_right, right_environment, row_sector
    )
    return raw.transpose(1, 0, 2), density


def solution(mesh):
    torus = Mesh(mesh.devices.reshape(2, 4, 2, 4, 2), AXES)
    in_specs = (P(LB, None, RB), P(None, LB, None), P(), P(), P(None, RB, LB), P())
    out_specs = (P(LB, None, RB), P(LB, RB))
    return jax.shard_map(
        shards, mesh=torus, in_specs=in_specs, out_specs=out_specs, check_vma=False
    )
```

```python
import functools
import math

import jax
import jax.numpy as jnp
from jax import lax
from jax.experimental import pallas as pl
from jax.experimental.pallas import tpu as pltpu
from jax.sharding import Mesh
from jax.sharding import PartitionSpec as P

BOND_WIDTH = 3072
SECTOR_TILES = 4
AXES = ("zl", "y", "core", "x", "zh")
LB = ("zl", "y", "core")
RB = ("x", "zh")
BF16, F32 = jnp.bfloat16, jnp.float32

MAIN, REST = 128, 64
PIECES = (
    (("z", 1, 0, 64), ("z", -1, 64, 48), ("y", 1, 112, 32), ("y", -1, 144, 48)),
    (("z", 1, 0, 32), ("z", -1, 32, 32), ("y", 1, 64, 32), ("y", -1, 96, 32)),
    (("z", 1, 0, 32), ("z", -1, 32, 16), ("y", -1, 48, 16)),
)
UNIT_BYTES = (1536 * 2, 8 * 384 * 2, 8 * 384 * 2)
SHARD = (192, MAIN, REST)
SOURCES = tuple((dz, dy) for dz in (0, 1) for dy in range(4))
MESSAGES = tuple(
    (phase, piece, source)
    for phase in range(3)
    for piece in range(len(PIECES[phase]))
    for source in SOURCES[1:]
)


FIRSTS = (((0, 0),), ((0, 1), (0, 3)), ((1, 0),), ((1, 1), (1, 3)), ((0, 2), (1, 2)))
LATER = (("away", 10.0), ("keep", 1.0), ("finish", 6.0), ("swap", 0.5), ("gram", 9.0))


def forwards(phase, piece, source):
    tree, turn = PIECES[phase][piece][:2]
    (dz, dy), on, back = source, "+-"[turn < 0], (-turn) % 4
    named = lambda link, place: (link, (phase, piece, place))
    if tree == "z":
        if source == (1, 0):
            return [named("+", (1, 3)), named("-", (1, 1))]
        return [named(on, (dz, 2))] if dy == back else []
    if dz:
        return []
    across = [named("z", (1, dy))]
    return [named(on, (0, 2)), *across] if dy == back else across


def own_sends():
    for phase in range(3):
        pieces = range(len(PIECES[phase]))
        for piece in sorted(pieces, key=lambda p: PIECES[phase][p][0] == "y"):
            yield "z", (phase, piece, (1, 0))
        for piece in sorted(pieces, key=lambda p: PIECES[phase][p][0] == "z"):
            yield "+", (phase, piece, (0, 3))
            yield "-", (phase, piece, (0, 1))


def schedule(rate=43.5e3, lag=1.0, lead=10.0, step=0.05):
    spent = (None, 1.1, 0.7)
    waiting = {link: [] for link in "+-z"}
    for order, (link, message) in enumerate(own_sends()):
        waiting[link].append((message[0], order, message, True))
    free_at = dict.fromkeys("+-z", 0.0)
    arriving, beside, done, ops, issued = [], [], set(), [], []
    pieces_left = {(p, s): len(PIECES[p]) for p in range(3) for s in SOURCES[1:]}
    ready = {(p, s): None for p in range(3) for s in SOURCES}
    for phase in range(3):
        ready[phase, (0, 0)] = 4.0 + phase
    firsts, mixes, seconds = 0, 0, [0, 0]
    later = []
    order, now, tc_free = 1000, 0.0, 0.0
    while seconds[1] < 8:
        now += step
        for link in "+-z":
            if free_at[link] <= now and waiting[link]:
                job = min(waiting[link])
                waiting[link].remove(job)
                phase, piece, _ = message = job[2]
                took = PIECES[phase][piece][3] * UNIT_BYTES[phase] / rate
                if job[3]:
                    issued.append((max(0.0, now - lead), len(issued), link, message))
                free_at[link] = now + took
                arriving.append((now + took + lag, message))
        if tc_free > now:
            continue
        landed = [entry for entry in arriving if entry[0] <= now]
        if landed:
            entry = min(landed)
            arriving.remove(entry)
            message = entry[1]
            onward = forwards(*message)
            for link, passed in onward:
                order += 1
                waiting[link].append((passed[0], order, passed, False))
            ops.append((now, "take", message, onward))
            phase, _, source = message
            pieces_left[phase, source] -= 1
            if not pieces_left[phase, source]:
                ops.append((now, "share", phase, source))
                size = SHARD[phase] * UNIT_BYTES[phase]
                ready[phase, source] = now + 2.0 + size / 400e3
            tc_free = now + 0.2
            continue
        able = [k for k, at in ready.items() if at is not None and at <= now and k not in done]
        group = FIRSTS[firsts] if firsts < len(FIRSTS) else None
        due = [entry for entry in later if entry[0] <= now]
        if due and due[0][1] == "first":
            later.remove(due[0])
            ops.append((now, *due[0][1:]))
            tc_free = now + 0.4 + 0.6 * len(due[0][2])
        elif group is not None:
            if all((0, source) in able for source in group):
                done.update((0, source) for source in group)
                for part in (0, 1):
                    later.append((now, "first", group, firsts == 0, part))
                firsts += 1
        elif mixes < 4:
            ops.append((now, "mix", mixes))
            mixes += 1
            tc_free = now + 1.1
        elif due:
            later.remove(due[0])
            ops.append((now, *due[0][1:]))
            tc_free = now + 0.7
        elif able:
            phase, source = min(able, key=lambda k: (k[0], ready[k]))
            done.add((phase, source))
            ops.append((now, "second", phase, source))
            seconds[phase - 1] += 1
            tc_free = now + spent[phase]
            if phase == 1 and seconds[0] == 8:
                wait = 0.0
                for name, gap in LATER:
                    wait += gap
                    later.append((tc_free + wait, name, 1))
    rest = [entry[1] for entry in later]
    ops += [(now, name, 1) for name in rest[:-1]]
    ops += [(now, name, 2) for name, _ in LATER[:-1]]
    ops += [(now, "gram", phase) for phase in ((1, 2) if rest else (2,))]
    for at, _, link, message in reversed(issued):
        place = next((i for i, op in enumerate(ops) if op[0] > at), len(ops))
        ops.insert(place, (at, "send", link, message))
    return [op[1:] for op in ops], now


OFFSETS = (1, 2, 3, -1, -2, -3)


def row_device(m):
    return {"zl": m // 8, "y": lax.rem(m // 2, 4), "core": lax.rem(m, 2)}


def column_device(n):
    return {"x": n // 2, "zh": lax.rem(n, 2)}


def inside(m):
    return jnp.logical_and(m >= 0, m < 16)


def ring(value, by, size):
    return lax.rem(value + (by % size), size)


def kernel(
    ops, w_ref, l_ref, r_ref, ol_ref, or_ref, sector_ref, out_ref, density_ref,
    raw, left, wide, main, rest, acc, mixed, coef, part_main, part_rest, from_main, from_rest,
    kept_main, kept_rest, away_main, away_rest, back_main, back_rest,
    tile_main, tile_rest, mates_main, mates_rest, grams, turned, turned_out, turned_in, blocks_out, blocks_in,
    local_sem, send_sem, recv_sem, share_send, share_recv, x_send, x_recv, z_send, z_recv,
    swap_send, swap_recv, turn_send, turn_recv, block_send, block_recv,
):
    zl, y, core, x, zh = (lax.axis_index(a) for a in AXES)
    gathered = (wide, main, rest)
    number = {m: i for i, m in enumerate(MESSAGES)}
    neighbour = {
        "+": {"y": ring(y, 1, 4)},
        "-": {"y": ring(y, -1, 4)},
        "z": {"zl": 1 - zl},
    }
    mesh_type = pl.DeviceIdType.MESH

    def chip(source):
        dz, dy = source
        return (1 - zl if dz else zl) * 4 + ring(y, dy, 4)

    barrier = pltpu.get_barrier_semaphore()
    here = chip((0, 0)) * 2 + core
    column = x * 2 + zh
    partners = [*neighbour.values(), {"core": 1 - core}]
    partners += [column_device(ring(column, by, 8)) for by in range(1, 8)]
    for partner in partners:
        pl.semaphore_signal(barrier, inc=1, device_id=partner, device_id_type=mesh_type)
    mates = jnp.int32(0)
    for offset in OFFSETS:
        mates += inside(here + offset).astype(jnp.int32)

        @pl.when(inside(here + offset))
        def _(offset=offset):
            pl.semaphore_signal(
                barrier, inc=1, device_id=row_device(here + offset), device_id_type=mesh_type
            )

    loads = [
        pltpu.make_async_copy(w_ref, raw, local_sem.at[0]),
        pltpu.make_async_copy(r_ref.at[:, 0:MAIN], main.at[here], local_sem.at[1]),
        pltpu.make_async_copy(r_ref.at[:, MAIN : MAIN + REST], rest.at[here], local_sem.at[2]),
        pltpu.make_async_copy(l_ref, left, local_sem.at[3]),
    ]
    for load in loads:
        load.start()
    loads[0].wait()
    wide[here] = raw[...].reshape(192, 1536)
    loads[1].wait()
    loads[2].wait()
    pl.semaphore_wait(barrier, len(partners) + mates)

    sent = []

    def piece_of(message, receiver):
        phase, piece, _ = message
        start, size = PIECES[phase][piece][2:]
        if phase == 0:
            return wide.at[receiver, pl.ds(start, size)]
        return gathered[phase].at[receiver, :, pl.ds(start, size)]

    def send(link, message, source):
        block = piece_of(message, chip(source) * 2 + core)
        at = number[message]
        copy = pltpu.make_async_remote_copy(
            block, block, send_sem.at[at], recv_sem.at[at],
            device_id=neighbour[link], device_id_type=mesh_type,
        )
        copy.start()
        sent.append(copy)

    def arrived(message):
        block = piece_of(message, chip(message[2]) * 2 + core)
        at = number[message]
        pltpu.make_async_remote_copy(
            block, block, send_sem.at[at], recv_sem.at[at],
            device_id=neighbour["z"], device_id_type=mesh_type,
        ).wait_recv()

    def share(phase, source, owner):
        at = phase * 8 + SOURCES.index(source)
        block = gathered[phase].at[chip(source) * 2 + owner]
        return pltpu.make_async_remote_copy(
            block, block, share_send.at[at], share_recv.at[at],
            device_id={"core": 1 - core}, device_id_type=mesh_type,
        )

    def coefficients():
        def of(size, dim):
            return lax.broadcasted_iota(jnp.int32, size, dim)

        def dot(a, b, dims=(((1,), (0,)), ((), ()))):
            return lax.dot_general(
                a, b, dims, precision=lax.Precision.HIGHEST, preferred_element_type=F32
            )

        across = (((1,), (1,)), ((), ()))
        tall, short = of((256, 32), 0), of((256, 32), 1)
        pick = (of((256, 8), 0) // 32 == of((256, 8), 1)).astype(F32)
        right = dot(pick, or_ref[...].reshape(32, 8), across)
        right = jnp.where(tall // 8 % 2 == short // 2 % 2, right, 0.0)
        i, j = of((32, 32), 0), of((32, 32), 1)
        right = dot(right, jnp.logical_and(i // 4 == j // 4, i % 2 == j % 2).astype(F32))
        right = jnp.where(tall // 16 % 2 == short // 2 % 2, right, 0.0)
        lefts = ol_ref[...].reshape(32, 8)
        total = None
        for site in (0, 1):
            wanted = jnp.logical_and(tall // 32 == short // 4, tall // 16 % 2 == short % 2)
            wanted = jnp.logical_and(wanted, short // 2 % 2 == site).astype(F32)
            i, j = of((8, 32), 0), of((8, 32), 1)
            place = jnp.logical_and(i == j // 4, j // 2 % 2 == site).astype(F32)
            term = dot(dot(wanted, lefts), place)
            total = term if total is None else total + term
        total = jnp.where(tall // 8 % 2 == short % 2, total, 0.0)
        full = dot(right, total, across)
        full = jnp.where(of((256, 256), 0) % 8 == of((256, 256), 1) % 8, full, 0.0)
        high = full.astype(BF16)
        coef[0:256] = high
        coef[256:512] = (full - high.astype(F32)).astype(BF16)

    def first(group, fresh, part):
        chips = [chip(source) for source in group]
        columns = [pl.ds(pl.multiple_of(k * 384, 384), 384) for k in chips]

        @pl.loop(part * 3, part * 3 + 3)
        def _(tile):
            lanes = pl.ds(pl.multiple_of(tile * 256, 256), 256)
            block = [wide[pl.ds(k * 2, 2), :, lanes].reshape(384, 256) for k in chips]
            rows = [left[:, c] for c in columns]
            product = jnp.dot(
                jnp.concatenate(rows, axis=1), jnp.concatenate(block, axis=0),
                preferred_element_type=F32,
            )
            if fresh:
                acc[:, lanes] = product
            else:
                acc[:, lanes] += product

    def mix(quarter):
        @pl.loop(quarter * 2, quarter * 2 + 2)
        def _(group):
            halves = []
            for sub in range(2):
                start = pl.multiple_of(group * 16 + sub * 8, 8)
                stack = jnp.concatenate(
                    [
                        acc[pl.ds(a * 128 + start, 8), s * 384 : s * 384 + 384]
                        for a in range(8)
                        for s in range(4)
                    ],
                    axis=0,
                )
                top = stack.astype(BF16)
                under = (stack - top.astype(F32)).astype(BF16)
                both = jnp.dot(coef[...], top, preferred_element_type=F32)
                third = jnp.dot(coef[0:256], under, preferred_element_type=F32)
                halves.append(both[0:256] + both[256:512] + third)
            for v in range(8):
                for out_site in range(4):
                    at = (v * 4 + out_site) * 8
                    value = jnp.concatenate([h[at : at + 8] for h in halves], axis=0)
                    rows = pl.ds(pl.multiple_of(out_site * 128 + group * 16, 16), 16)
                    mixed[rows, v * 384 : v * 384 + 384] = value.astype(BF16)

    parts, froms = (None, part_main, part_rest), (None, from_main, from_rest)
    keeps, aways, backs = (None, kept_main, kept_rest), (None, away_main, away_rest), (None, back_main, back_rest)

    def to_owner(phase, k):
        owner, half = k // 2, lax.rem(k, 2)
        slot = lax.rem(x - owner + 7, 4)
        slot = jnp.minimum(slot, 2)
        copy = pltpu.make_async_remote_copy(
            parts[phase].at[k], froms[phase].at[half, slot],
            x_send.at[(phase - 1) * 8 + k], x_recv.at[(phase - 1) * 6 + half * 3 + slot],
            device_id={"x": owner}, device_id_type=mesh_type,
        )
        return copy, x != owner

    def second(phase, source):
        k = chip(source)
        width = 2 * SHARD[phase]

        total = None
        for v in range(0, 8, 2):
            block = [gathered[phase][pl.ds(k * 2, 2), v + j].reshape(width, 384) for j in (0, 1)]
            product = lax.dot_general(
                mixed[:, v * 384 : v * 384 + 768], jnp.concatenate(block, axis=1),
                (((1,), (1,)), ((), ())), preferred_element_type=F32,
            )
            total = product if total is None else total + product
        parts[phase][k] = total.astype(BF16)

        copy, away = to_owner(phase, k)

        @pl.when(away)
        def _():
            copy.start()

    def z_copy(phase):
        return pltpu.make_async_remote_copy(
            aways[phase], backs[phase], z_send.at[phase - 1], z_recv.at[phase - 1],
            device_id={"zh": 1 - zh}, device_id_type=mesh_type,
        )

    def sum_x(phase, half, put):
        for slot in range(3):
            pltpu.make_async_remote_copy(
                parts[phase].at[0], froms[phase].at[half, slot],
                x_send.at[0], x_recv.at[(phase - 1) * 6 + half * 3 + slot],
                device_id={"x": ring(x, 1, 4)}, device_id_type=mesh_type,
            ).wait_recv()

        @pl.loop(0, 8)
        def _(tile):
            rows = pl.ds(pl.multiple_of(tile * 64, 64), 64)
            total = parts[phase][x * 2 + half, rows].astype(F32)
            for slot in range(3):
                total += froms[phase][half, slot, rows].astype(F32)
            put(rows, total)

    def sum_away(phase):
        def put(rows, total):
            aways[phase][rows] = total.astype(BF16)

        sum_x(phase, 1 - zh, put)
        z_copy(phase).start()

    def sum_keep(phase):
        def put(rows, total):
            keeps[phase][rows] = total

        sum_x(phase, zh, put)

    tiles = (None, tile_main, tile_rest)
    mates_of = (None, mates_main, mates_rest)

    def finish(phase):
        z_copy(phase).wait_recv()
        for site in range(4):
            rows = slice(site * 128, site * 128 + 128)
            value = keeps[phase][rows] + backs[phase][rows].astype(F32)
            keeps[phase][rows] = value
            tiles[phase][site] = value.astype(BF16)

    def swap(phase, offset):
        half, at = int(offset > 0), abs(offset) - 1
        slot = ((phase - 1) * 2 + half) * 3 + at
        return pltpu.make_async_remote_copy(
            tiles[phase].at[pl.ds(half * 2, 2)], mates_of[phase].at[half, at],
            swap_send.at[slot], swap_recv.at[slot],
            device_id=row_device(here + offset), device_id_type=mesh_type,
        )

    def nt(a, b):
        return lax.dot_general(a, b, (((1,), (1,)), ((), ())), preferred_element_type=F32)

    def swaps(phase):
        for offset in OFFSETS:

            @pl.when(inside(here + offset))
            def _(offset=offset):
                swap(phase, offset).start()

        tile = jnp.concatenate([tiles[phase][site] for site in range(4)], axis=1)
        own = nt(tile, tile)
        grams[2, :, 0:128] = own if phase == 1 else grams[2, :, 0:128] + own

    def gram(phase):
        width = 2 * SHARD[phase]
        for half in (0, 1):
            for offset in OFFSETS[3 - 3 * half :][:3]:

                @pl.when(inside(here - offset))
                def _(offset=offset):
                    swap(phase, offset).wait_recv()

            mine = jnp.concatenate([tiles[phase][half * 2 + j] for j in (0, 1)], axis=1)
            theirs = [mates_of[phase][half, :, j].reshape(384, width) for j in (0, 1)]
            theirs = jnp.concatenate(theirs, axis=1)
            straight, crossed = nt(mine, theirs), nt(theirs, mine)
            if phase == 1:
                grams[half] = straight
                turned[half] = crossed
            else:
                turned_out[half] = (turned[half] + crossed).astype(BF16)
                grams[half] += straight
                for offset in OFFSETS[3 * half :][:3]:

                    @pl.when(inside(here + offset))
                    def _(offset=offset):
                        turn(offset).start()

    def turn(offset):
        half, at = int(offset < 0), abs(offset) - 1
        return pltpu.make_async_remote_copy(
            turned_out.at[half, pl.ds(at * 128, 128)], turned_in.at[1 - half, pl.ds(at * 128, 128)],
            turn_send.at[half * 3 + at], turn_recv.at[half * 3 + at],
            device_id=row_device(here + offset), device_id_type=mesh_type,
        )

    def block_copy(offset):
        mate = here + offset
        owner, half = mate // 2, lax.rem(mate, 2)
        return pltpu.make_async_remote_copy(
            blocks_out.at[offset + 3], blocks_in.at[half, column],
            block_send.at[offset + 3], block_recv.at[half * 8 + column],
            device_id=column_device(owner), device_id_type=mesh_type,
        )

    def reach():
        for offset in (0, *OFFSETS):
            half, at = int(offset < 0), abs(offset) - 1

            @pl.when(inside(here + offset))
            def _(offset=offset, half=half, at=at):
                if offset:
                    turn(-offset).wait_recv()
                    came = turned_in[half, at * 128 : at * 128 + 128].astype(F32)
                    value = grams[half, :, at * 128 : at * 128 + 128] + came
                else:
                    value = grams[2, :, 0:128]
                owner = (here + offset) // 2

                @pl.when(owner == column)
                def _():
                    blocks_in[lax.rem(here + offset, 2), column] = value.astype(BF16)

                @pl.when(owner != column)
                def _():
                    blocks_out[offset + 3] = value.astype(BF16)
                    block_copy(offset).start()

        for half in (0, 1):
            mate = column * 2 + half
            near = jnp.logical_and(mate - here <= 3, here - mate <= 3)
            lanes = slice(half * 128, half * 128 + 128)

            @pl.when(near)
            def _(half=half, mate=mate, lanes=lanes):
                for by in range(1, 8):
                    source = ring(column, by, 8)
                    pltpu.make_async_remote_copy(
                        blocks_out.at[0], blocks_in.at[half, source],
                        block_send.at[0], block_recv.at[half * 8 + source],
                        device_id=column_device(source), device_id_type=mesh_type,
                    ).wait_recv()
                total = sum(blocks_in[half, n].astype(F32) for n in range(8))
                same_sector = sector_ref[mate] == sector_ref[here]
                total = total * (1.0 / math.sqrt(4.0 * BOND_WIDTH))
                density_ref[:, lanes] = jnp.where(same_sector, total, 0.0)

            @pl.when(jnp.logical_not(near))
            def _(lanes=lanes):
                density_ref[:, lanes] = jnp.zeros((128, 128), F32)

    def write_out():
        lane = lax.broadcasted_iota(jnp.int32, (128, 128), 1)
        for site in range(4):
            rows = slice(site * 128, site * 128 + 128)
            out_ref[site, :, 0:128] = tile_main[site, :, 0:128]
            rolled = pltpu.roll(kept_main[rows, 128:256], 64, 1)
            last = kept_rest[rows, :]
            out_ref[site, :, 128:256] = jnp.where(lane < 64, last, rolled).astype(BF16)
            out_ref[site, :, 256:384] = jnp.where(lane < 64, rolled, last).astype(BF16)

    after = dict(away=sum_away, keep=sum_keep, finish=finish, swap=swaps, gram=gram)
    for phase in range(3):
        share(phase, (0, 0), core).start()
    for op in ops:
        if op[0] == "first" and op[2] and not op[3]:
            coefficients()
        if op[0] == "send":
            send(op[1], op[2], (0, 0))
        elif op[0] == "take":
            arrived(op[1])
            for link, passed in op[2]:
                send(link, passed, op[1][2])
        elif op[0] == "share":
            share(op[1], op[2], core).start()
        elif op[0] == "first":
            if not op[3]:
                for source in op[1]:
                    share(0, source, 1 - core).wait_recv()
            if op[2] and not op[3]:
                loads[3].wait()
            first(*op[1:])
        elif op[0] == "mix":
            mix(op[1])
        elif op[0] == "second":
            share(op[1], op[2], 1 - core).wait_recv()
            second(op[1], op[2])
        else:
            if op == ("gram", 2):
                write_out()
            after[op[0]](op[1])
    reach()
    for copy in sent:
        copy.wait_send()
    for phase in range(3):
        for source in SOURCES:
            share(phase, source, core).wait_send()
    for phase in (1, 2):
        z_copy(phase).wait_send()
        for k in range(8):
            copy, away = to_owner(phase, k)

            @pl.when(away)
            def _(copy=copy):
                copy.wait_send()

    for offset in OFFSETS:

        @pl.when(inside(here + offset))
        def _(offset=offset):
            swap(1, offset).wait_send()
            swap(2, offset).wait_send()
            turn(offset).wait_send()

    for offset in (0, *OFFSETS):

        @pl.when(jnp.logical_and(inside(here + offset), (here + offset) // 2 != column))
        def _(offset=offset):
            block_copy(offset).wait_send()


def fused(wavefunction, left_environment, operator_left, operator_right, right_environment, row_sector):
    ops, _ = schedule()
    vmem = pltpu.VMEM
    dma = pltpu.SemaphoreType.DMA
    count = len(MESSAGES)
    scratch = [
        vmem((192, 4, 384), BF16), vmem((1024, 3072), BF16), vmem((16, 192, 1536), BF16), vmem((16, 8, MAIN, 384), BF16),
        vmem((16, 8, REST, 384), BF16), vmem((1024, 1536), F32), vmem((512, 3072), BF16),
        vmem((512, 256), BF16), vmem((8, 512, 256), BF16), vmem((8, 512, 128), BF16),
        vmem((2, 3, 512, 256), BF16), vmem((2, 3, 512, 128), BF16),
        vmem((512, 256), F32), vmem((512, 128), F32), vmem((512, 256), BF16), vmem((512, 128), BF16),
        vmem((512, 256), BF16), vmem((512, 128), BF16),
        vmem((4, 128, 256), BF16), vmem((4, 128, 128), BF16), vmem((2, 3, 2, 128, 256), BF16),
        vmem((2, 3, 2, 128, 128), BF16), vmem((3, 128, 384), F32), vmem((2, 384, 128), F32),
        vmem((2, 384, 128), BF16), vmem((2, 384, 128), BF16), vmem((7, 128, 128), BF16),
        vmem((2, 8, 128, 128), BF16),
        dma((4,)), dma((count,)), dma((count,)), dma((24,)), dma((24,)), dma((16,)), dma((12,)),
        dma((2,)), dma((2,)), dma((12,)), dma((12,)), dma((6,)), dma((6,)), dma((7,)), dma((16,)),
    ]
    spec = pl.BlockSpec(memory_space=pl.ANY)
    return pl.pallas_call(
        functools.partial(kernel, ops),
        out_shape=(pltpu.VMEM((4, 128, 384), BF16), pltpu.VMEM((128, 256), F32)),
        in_specs=[spec] * 3 + [pl.BlockSpec(memory_space=pltpu.VMEM)] * 2
        + [pl.BlockSpec(memory_space=pltpu.SMEM)],
        out_specs=(pl.BlockSpec(memory_space=pltpu.VMEM),) * 2,
        scratch_shapes=scratch,
        compiler_params=pltpu.CompilerParams(
            collective_id=0, has_side_effects=True, vmem_limit_bytes=61 << 20
        ),
    )(
        wavefunction,
        left_environment.reshape(1024, 3072),
        right_environment.transpose(0, 2, 1),
        operator_left.transpose(0, 2, 3, 1),
        operator_right.transpose(0, 2, 3, 1),
        row_sector,
    )


def shards(
    wavefunction, left_environment, operator_left, operator_right, right_environment, row_sector
):
    raw, density = fused(
        wavefunction, left_environment, operator_left, operator_right, right_environment, row_sector
    )
    return raw.transpose(1, 0, 2), density


def solution(mesh):
    torus = Mesh(mesh.devices.reshape(2, 4, 2, 4, 2), AXES)
    in_specs = (P(LB, None, RB), P(None, LB, None), P(), P(), P(None, RB, LB), P())
    out_specs = (P(LB, None, RB), P(LB, RB))
    return jax.shard_map(
        shards, mesh=torus, in_specs=in_specs, out_specs=out_specs, check_vma=False
    )
```

```python
import functools
import math

import jax
import jax.numpy as jnp
from jax import lax
from jax.experimental import pallas as pl
from jax.experimental.pallas import tpu as pltpu
from jax.sharding import Mesh
from jax.sharding import PartitionSpec as P

BOND_WIDTH = 3072
SECTOR_TILES = 4
AXES = ("zl", "y", "core", "x", "zh")
LB = ("zl", "y", "core")
RB = ("x", "zh")
BF16, F32 = jnp.bfloat16, jnp.float32

MAIN, REST = 128, 64
PIECES = (
    (("z", 1, 0, 64), ("z", -1, 64, 48), ("y", 1, 112, 32), ("y", -1, 144, 48)),
    (("z", 1, 0, 32), ("z", -1, 32, 32), ("y", 1, 64, 32), ("y", -1, 96, 32)),
    (("z", 1, 0, 32), ("z", -1, 32, 16), ("y", -1, 48, 16)),
)
UNIT_BYTES = (1536 * 2, 8 * 384 * 2, 8 * 384 * 2)
SHARD = (192, MAIN, REST)
SOURCES = tuple((dz, dy) for dz in (0, 1) for dy in range(4))
MESSAGES = tuple(
    (phase, piece, source)
    for phase in range(3)
    for piece in range(len(PIECES[phase]))
    for source in SOURCES[1:]
)


FIRSTS = (((0, 0),), ((0, 1), (0, 3)), ((1, 0),), ((1, 1), (1, 3)), ((0, 2), (1, 2)))
LATER = (("away", 15.0), ("keep", 1.0), ("finish", 6.0), ("swap", 0.5), ("gram", 9.0))


def forwards(phase, piece, source):
    tree, turn = PIECES[phase][piece][:2]
    (dz, dy), on, back = source, "+-"[turn < 0], (-turn) % 4
    named = lambda link, place: (link, (phase, piece, place))
    if tree == "z":
        if source == (1, 0):
            return [named("+", (1, 3)), named("-", (1, 1))]
        return [named(on, (dz, 2))] if dy == back else []
    if dz:
        return []
    across = [named("z", (1, dy))]
    return [named(on, (0, 2)), *across] if dy == back else across


def own_sends():
    for phase in range(3):
        pieces = range(len(PIECES[phase]))
        for piece in sorted(pieces, key=lambda p: PIECES[phase][p][0] == "y"):
            yield "z", (phase, piece, (1, 0))
        for piece in sorted(pieces, key=lambda p: PIECES[phase][p][0] == "z"):
            yield "+", (phase, piece, (0, 3))
            yield "-", (phase, piece, (0, 1))


def schedule(rate=41e3, lag=3.0, lead=10.0, step=0.05):
    spent = (None, 1.1, 0.7)
    waiting = {link: [] for link in "+-z"}
    for order, (link, message) in enumerate(own_sends()):
        waiting[link].append((message[0], order, message, True))
    free_at = dict.fromkeys("+-z", 0.0)
    arriving, beside, done, ops, issued = [], [], set(), [], []
    pieces_left = {(p, s): len(PIECES[p]) for p in range(3) for s in SOURCES[1:]}
    ready = {(p, s): None for p in range(3) for s in SOURCES}
    for phase in range(3):
        ready[phase, (0, 0)] = 4.0 + phase
    firsts, mixes, seconds = 0, 0, [0, 0]
    later = []
    order, now, tc_free = 1000, 0.0, 0.0
    while seconds[1] < 8:
        now += step
        for link in "+-z":
            if free_at[link] <= now and waiting[link]:
                job = min(waiting[link])
                waiting[link].remove(job)
                phase, piece, _ = message = job[2]
                took = PIECES[phase][piece][3] * UNIT_BYTES[phase] / rate
                if job[3]:
                    issued.append((max(0.0, now - lead), len(issued), link, message))
                free_at[link] = now + took
                arriving.append((now + took + lag, message))
        if tc_free > now:
            continue
        landed = [entry for entry in arriving if entry[0] <= now]
        if landed:
            entry = min(landed)
            arriving.remove(entry)
            message = entry[1]
            onward = forwards(*message)
            for link, passed in onward:
                order += 1
                waiting[link].append((passed[0], order, passed, False))
            ops.append((now, "take", message, onward))
            phase, _, source = message
            pieces_left[phase, source] -= 1
            if not pieces_left[phase, source]:
                ops.append((now, "share", phase, source))
                size = SHARD[phase] * UNIT_BYTES[phase]
                ready[phase, source] = now + 2.0 + size / 400e3
            tc_free = now + 0.2
            continue
        able = [k for k, at in ready.items() if at is not None and at <= now and k not in done]
        group = FIRSTS[firsts] if firsts < len(FIRSTS) else None
        due = [entry for entry in later if entry[0] <= now]
        if due and due[0][1] == "first":
            later.remove(due[0])
            ops.append((now, *due[0][1:]))
            tc_free = now + 0.4 + 0.6 * len(due[0][2])
        elif group is not None:
            if all((0, source) in able for source in group):
                done.update((0, source) for source in group)
                for part in (0, 1):
                    later.append((now, "first", group, firsts == 0, part))
                firsts += 1
        elif mixes < 4:
            ops.append((now, "mix", mixes))
            mixes += 1
            tc_free = now + 1.1
        elif due:
            later.remove(due[0])
            ops.append((now, *due[0][1:]))
            tc_free = now + 0.7
        elif able:
            phase, source = min(able, key=lambda k: (k[0], ready[k]))
            done.add((phase, source))
            ops.append((now, "second", phase, source))
            seconds[phase - 1] += 1
            tc_free = now + spent[phase]
            if phase == 1 and seconds[0] == 8:
                wait = 0.0
                for name, gap in LATER:
                    wait += gap
                    later.append((tc_free + wait, name, 1))
    rest = [entry[1] for entry in later]
    ops += [(now, name, 1) for name in rest[:-1]]
    ops += [(now, name, 2) for name, _ in LATER[:-1]]
    ops += [(now, "gram", phase) for phase in ((1, 2) if rest else (2,))]
    for at, _, link, message in reversed(issued):
        place = next((i for i, op in enumerate(ops) if op[0] > at), len(ops))
        ops.insert(place, (at, "send", link, message))
    return [op[1:] for op in ops], now


OFFSETS = (1, 2, 3, -1, -2, -3)


def row_device(m):
    return {"zl": m // 8, "y": lax.rem(m // 2, 4), "core": lax.rem(m, 2)}


def column_device(n):
    return {"x": n // 2, "zh": lax.rem(n, 2)}


def inside(m):
    return jnp.logical_and(m >= 0, m < 16)


def ring(value, by, size):
    return lax.rem(value + (by % size), size)


def kernel(
    ops, w_ref, l_ref, r_ref, ol_ref, or_ref, sector_ref, out_ref, density_ref,
    raw, left, wide, main, rest, acc, mixed, coef, part_main, part_rest, from_main, from_rest,
    kept_main, kept_rest, away_main, away_rest, back_main, back_rest,
    tile_main, tile_rest, mates_main, mates_rest, grams, turned, turned_out, turned_in, blocks_out, blocks_in,
    local_sem, send_sem, recv_sem, share_send, share_recv, x_send, x_recv, z_send, z_recv,
    swap_send, swap_recv, turn_send, turn_recv, block_send, block_recv,
):
    zl, y, core, x, zh = (lax.axis_index(a) for a in AXES)
    gathered = (wide, main, rest)
    number = {m: i for i, m in enumerate(MESSAGES)}
    neighbour = {
        "+": {"y": ring(y, 1, 4)},
        "-": {"y": ring(y, -1, 4)},
        "z": {"zl": 1 - zl},
    }
    mesh_type = pl.DeviceIdType.MESH

    def chip(source):
        dz, dy = source
        return (1 - zl if dz else zl) * 4 + ring(y, dy, 4)

    barrier = pltpu.get_barrier_semaphore()
    here = chip((0, 0)) * 2 + core
    column = x * 2 + zh
    partners = [*neighbour.values(), {"core": 1 - core}]
    partners += [column_device(ring(column, by, 8)) for by in range(1, 8)]
    for partner in partners:
        pl.semaphore_signal(barrier, inc=1, device_id=partner, device_id_type=mesh_type)
    mates = jnp.int32(0)
    for offset in OFFSETS:
        mates += inside(here + offset).astype(jnp.int32)

        @pl.when(inside(here + offset))
        def _(offset=offset):
            pl.semaphore_signal(
                barrier, inc=1, device_id=row_device(here + offset), device_id_type=mesh_type
            )

    loads = [
        pltpu.make_async_copy(w_ref, raw, local_sem.at[0]),
        pltpu.make_async_copy(r_ref.at[:, 0:MAIN], main.at[here], local_sem.at[1]),
        pltpu.make_async_copy(r_ref.at[:, MAIN : MAIN + REST], rest.at[here], local_sem.at[2]),
        pltpu.make_async_copy(l_ref, left, local_sem.at[3]),
    ]
    for load in loads:
        load.start()
    loads[0].wait()
    wide[here] = raw[...].reshape(192, 1536)
    loads[1].wait()
    loads[2].wait()
    pl.semaphore_wait(barrier, len(partners) + mates)

    sent = []

    def piece_of(message, receiver):
        phase, piece, _ = message
        start, size = PIECES[phase][piece][2:]
        if phase == 0:
            return wide.at[receiver, pl.ds(start, size)]
        return gathered[phase].at[receiver, :, pl.ds(start, size)]

    def send(link, message, source):
        block = piece_of(message, chip(source) * 2 + core)
        at = number[message]
        copy = pltpu.make_async_remote_copy(
            block, block, send_sem.at[at], recv_sem.at[at],
            device_id=neighbour[link], device_id_type=mesh_type,
        )
        copy.start()
        sent.append(copy)

    def arrived(message):
        block = piece_of(message, chip(message[2]) * 2 + core)
        at = number[message]
        pltpu.make_async_remote_copy(
            block, block, send_sem.at[at], recv_sem.at[at],
            device_id=neighbour["z"], device_id_type=mesh_type,
        ).wait_recv()

    def share(phase, source, owner):
        at = phase * 8 + SOURCES.index(source)
        block = gathered[phase].at[chip(source) * 2 + owner]
        return pltpu.make_async_remote_copy(
            block, block, share_send.at[at], share_recv.at[at],
            device_id={"core": 1 - core}, device_id_type=mesh_type,
        )

    def coefficients():
        def of(size, dim):
            return lax.broadcasted_iota(jnp.int32, size, dim)

        def dot(a, b, dims=(((1,), (0,)), ((), ()))):
            return lax.dot_general(
                a, b, dims, precision=lax.Precision.HIGHEST, preferred_element_type=F32
            )

        across = (((1,), (1,)), ((), ()))
        tall, short = of((256, 32), 0), of((256, 32), 1)
        pick = (of((256, 8), 0) // 32 == of((256, 8), 1)).astype(F32)
        right = dot(pick, or_ref[...].reshape(32, 8), across)
        right = jnp.where(tall // 8 % 2 == short // 2 % 2, right, 0.0)
        i, j = of((32, 32), 0), of((32, 32), 1)
        right = dot(right, jnp.logical_and(i // 4 == j // 4, i % 2 == j % 2).astype(F32))
        right = jnp.where(tall // 16 % 2 == short // 2 % 2, right, 0.0)
        lefts = ol_ref[...].reshape(32, 8)
        total = None
        for site in (0, 1):
            wanted = jnp.logical_and(tall // 32 == short // 4, tall // 16 % 2 == short % 2)
            wanted = jnp.logical_and(wanted, short // 2 % 2 == site).astype(F32)
            i, j = of((8, 32), 0), of((8, 32), 1)
            place = jnp.logical_and(i == j // 4, j // 2 % 2 == site).astype(F32)
            term = dot(dot(wanted, lefts), place)
            total = term if total is None else total + term
        total = jnp.where(tall // 8 % 2 == short % 2, total, 0.0)
        full = dot(right, total, across)
        full = jnp.where(of((256, 256), 0) % 8 == of((256, 256), 1) % 8, full, 0.0)
        high = full.astype(BF16)
        coef[0:256] = high
        coef[256:512] = (full - high.astype(F32)).astype(BF16)

    def first(group, fresh, part):
        chips = [chip(source) for source in group]
        columns = [pl.ds(pl.multiple_of(k * 384, 384), 384) for k in chips]

        @pl.loop(part * 3, part * 3 + 3)
        def _(tile):
            lanes = pl.ds(pl.multiple_of(tile * 256, 256), 256)
            block = [wide[pl.ds(k * 2, 2), :, lanes].reshape(384, 256) for k in chips]
            rows = [left[:, c] for c in columns]
            product = jnp.dot(
                jnp.concatenate(rows, axis=1), jnp.concatenate(block, axis=0),
                preferred_element_type=F32,
            )
            if fresh:
                acc[:, lanes] = product
            else:
                acc[:, lanes] += product

    def mix(quarter):
        @pl.loop(quarter * 2, quarter * 2 + 2)
        def _(group):
            halves = []
            for sub in range(2):
                start = pl.multiple_of(group * 16 + sub * 8, 8)
                stack = jnp.concatenate(
                    [
                        acc[pl.ds(a * 128 + start, 8), s * 384 : s * 384 + 384]
                        for a in range(8)
                        for s in range(4)
                    ],
                    axis=0,
                )
                top = stack.astype(BF16)
                under = (stack - top.astype(F32)).astype(BF16)
                both = jnp.dot(coef[...], top, preferred_element_type=F32)
                third = jnp.dot(coef[0:256], under, preferred_element_type=F32)
                halves.append(both[0:256] + both[256:512] + third)
            for v in range(8):
                for out_site in range(4):
                    at = (v * 4 + out_site) * 8
                    value = jnp.concatenate([h[at : at + 8] for h in halves], axis=0)
                    rows = pl.ds(pl.multiple_of(out_site * 128 + group * 16, 16), 16)
                    mixed[rows, v * 384 : v * 384 + 384] = value.astype(BF16)

    parts, froms = (None, part_main, part_rest), (None, from_main, from_rest)
    keeps, aways, backs = (None, kept_main, kept_rest), (None, away_main, away_rest), (None, back_main, back_rest)

    def to_owner(phase, k):
        owner, half = k // 2, lax.rem(k, 2)
        slot = lax.rem(x - owner + 7, 4)
        slot = jnp.minimum(slot, 2)
        copy = pltpu.make_async_remote_copy(
            parts[phase].at[k], froms[phase].at[half, slot],
            x_send.at[(phase - 1) * 8 + k], x_recv.at[(phase - 1) * 6 + half * 3 + slot],
            device_id={"x": owner}, device_id_type=mesh_type,
        )
        return copy, x != owner

    def second(phase, source):
        k = chip(source)
        width = 2 * SHARD[phase]

        total = None
        for v in range(0, 8, 2):
            block = [gathered[phase][pl.ds(k * 2, 2), v + j].reshape(width, 384) for j in (0, 1)]
            product = lax.dot_general(
                mixed[:, v * 384 : v * 384 + 768], jnp.concatenate(block, axis=1),
                (((1,), (1,)), ((), ())), preferred_element_type=F32,
            )
            total = product if total is None else total + product
        parts[phase][k] = total.astype(BF16)

        copy, away = to_owner(phase, k)

        @pl.when(away)
        def _():
            copy.start()

    def z_copy(phase):
        return pltpu.make_async_remote_copy(
            aways[phase], backs[phase], z_send.at[phase - 1], z_recv.at[phase - 1],
            device_id={"zh": 1 - zh}, device_id_type=mesh_type,
        )

    def sum_x(phase, half, put):
        for slot in range(3):
            pltpu.make_async_remote_copy(
                parts[phase].at[0], froms[phase].at[half, slot],
                x_send.at[0], x_recv.at[(phase - 1) * 6 + half * 3 + slot],
                device_id={"x": ring(x, 1, 4)}, device_id_type=mesh_type,
            ).wait_recv()

        @pl.loop(0, 8)
        def _(tile):
            rows = pl.ds(pl.multiple_of(tile * 64, 64), 64)
            total = parts[phase][x * 2 + half, rows].astype(F32)
            for slot in range(3):
                total += froms[phase][half, slot, rows].astype(F32)
            put(rows, total)

    def sum_away(phase):
        def put(rows, total):
            aways[phase][rows] = total.astype(BF16)

        sum_x(phase, 1 - zh, put)
        z_copy(phase).start()

    def sum_keep(phase):
        def put(rows, total):
            keeps[phase][rows] = total

        sum_x(phase, zh, put)

    tiles = (None, tile_main, tile_rest)
    mates_of = (None, mates_main, mates_rest)

    def finish(phase):
        z_copy(phase).wait_recv()
        for site in range(4):
            rows = slice(site * 128, site * 128 + 128)
            value = keeps[phase][rows] + backs[phase][rows].astype(F32)
            keeps[phase][rows] = value
            tiles[phase][site] = value.astype(BF16)

    def swap(phase, offset):
        half, at = int(offset > 0), abs(offset) - 1
        slot = ((phase - 1) * 2 + half) * 3 + at
        return pltpu.make_async_remote_copy(
            tiles[phase].at[pl.ds(half * 2, 2)], mates_of[phase].at[half, at],
            swap_send.at[slot], swap_recv.at[slot],
            device_id=row_device(here + offset), device_id_type=mesh_type,
        )

    def nt(a, b):
        return lax.dot_general(a, b, (((1,), (1,)), ((), ())), preferred_element_type=F32)

    def swaps(phase):
        for offset in OFFSETS:

            @pl.when(inside(here + offset))
            def _(offset=offset):
                swap(phase, offset).start()

        tile = jnp.concatenate([tiles[phase][site] for site in range(4)], axis=1)
        own = nt(tile, tile)
        grams[2, :, 0:128] = own if phase == 1 else grams[2, :, 0:128] + own

    def gram(phase):
        width = 2 * SHARD[phase]
        for half in (0, 1):
            for offset in OFFSETS[3 - 3 * half :][:3]:

                @pl.when(inside(here - offset))
                def _(offset=offset):
                    swap(phase, offset).wait_recv()

            mine = jnp.concatenate([tiles[phase][half * 2 + j] for j in (0, 1)], axis=1)
            theirs = [mates_of[phase][half, :, j].reshape(384, width) for j in (0, 1)]
            theirs = jnp.concatenate(theirs, axis=1)
            straight, crossed = nt(mine, theirs), nt(theirs, mine)
            if phase == 1:
                grams[half] = straight
                turned[half] = crossed
            else:
                turned_out[half] = (turned[half] + crossed).astype(BF16)
                grams[half] += straight
                for offset in OFFSETS[3 * half :][:3]:

                    @pl.when(inside(here + offset))
                    def _(offset=offset):
                        turn(offset).start()

    def turn(offset):
        half, at = int(offset < 0), abs(offset) - 1
        return pltpu.make_async_remote_copy(
            turned_out.at[half, pl.ds(at * 128, 128)], turned_in.at[1 - half, pl.ds(at * 128, 128)],
            turn_send.at[half * 3 + at], turn_recv.at[half * 3 + at],
            device_id=row_device(here + offset), device_id_type=mesh_type,
        )

    def block_copy(offset):
        mate = here + offset
        owner, half = mate // 2, lax.rem(mate, 2)
        return pltpu.make_async_remote_copy(
            blocks_out.at[offset + 3], blocks_in.at[half, column],
            block_send.at[offset + 3], block_recv.at[half * 8 + column],
            device_id=column_device(owner), device_id_type=mesh_type,
        )

    def reach():
        for offset in (0, *OFFSETS):
            half, at = int(offset < 0), abs(offset) - 1

            @pl.when(inside(here + offset))
            def _(offset=offset, half=half, at=at):
                if offset:
                    turn(-offset).wait_recv()
                    came = turned_in[half, at * 128 : at * 128 + 128].astype(F32)
                    value = grams[half, :, at * 128 : at * 128 + 128] + came
                else:
                    value = grams[2, :, 0:128]
                owner = (here + offset) // 2

                @pl.when(owner == column)
                def _():
                    blocks_in[lax.rem(here + offset, 2), column] = value.astype(BF16)

                @pl.when(owner != column)
                def _():
                    blocks_out[offset + 3] = value.astype(BF16)
                    block_copy(offset).start()

        for half in (0, 1):
            mate = column * 2 + half
            near = jnp.logical_and(mate - here <= 3, here - mate <= 3)
            lanes = slice(half * 128, half * 128 + 128)

            @pl.when(near)
            def _(half=half, mate=mate, lanes=lanes):
                for by in range(1, 8):
                    source = ring(column, by, 8)
                    pltpu.make_async_remote_copy(
                        blocks_out.at[0], blocks_in.at[half, source],
                        block_send.at[0], block_recv.at[half * 8 + source],
                        device_id=column_device(source), device_id_type=mesh_type,
                    ).wait_recv()
                total = sum(blocks_in[half, n].astype(F32) for n in range(8))
                same_sector = sector_ref[mate] == sector_ref[here]
                total = total * (1.0 / math.sqrt(4.0 * BOND_WIDTH))
                density_ref[:, lanes] = jnp.where(same_sector, total, 0.0)

            @pl.when(jnp.logical_not(near))
            def _(lanes=lanes):
                density_ref[:, lanes] = jnp.zeros((128, 128), F32)

    def write_out():
        lane = lax.broadcasted_iota(jnp.int32, (128, 128), 1)
        for site in range(4):
            rows = slice(site * 128, site * 128 + 128)
            out_ref[site, :, 0:128] = tile_main[site, :, 0:128]
            rolled = pltpu.roll(kept_main[rows, 128:256], 64, 1)
            last = kept_rest[rows, :]
            out_ref[site, :, 128:256] = jnp.where(lane < 64, last, rolled).astype(BF16)
            out_ref[site, :, 256:384] = jnp.where(lane < 64, rolled, last).astype(BF16)

    after = dict(away=sum_away, keep=sum_keep, finish=finish, swap=swaps, gram=gram)
    for phase in range(3):
        share(phase, (0, 0), core).start()
    for op in ops:
        if op[0] == "first" and op[2] and not op[3]:
            coefficients()
        if op[0] == "send":
            send(op[1], op[2], (0, 0))
        elif op[0] == "take":
            arrived(op[1])
            for link, passed in op[2]:
                send(link, passed, op[1][2])
        elif op[0] == "share":
            share(op[1], op[2], core).start()
        elif op[0] == "first":
            if not op[3]:
                for source in op[1]:
                    share(0, source, 1 - core).wait_recv()
            if op[2] and not op[3]:
                loads[3].wait()
            first(*op[1:])
        elif op[0] == "mix":
            mix(op[1])
        elif op[0] == "second":
            share(op[1], op[2], 1 - core).wait_recv()
            second(op[1], op[2])
        else:
            if op == ("gram", 2):
                write_out()
            after[op[0]](op[1])
    reach()
    for copy in sent:
        copy.wait_send()
    for phase in range(3):
        for source in SOURCES:
            share(phase, source, core).wait_send()
    for phase in (1, 2):
        z_copy(phase).wait_send()
        for k in range(8):
            copy, away = to_owner(phase, k)

            @pl.when(away)
            def _(copy=copy):
                copy.wait_send()

    for offset in OFFSETS:

        @pl.when(inside(here + offset))
        def _(offset=offset):
            swap(1, offset).wait_send()
            swap(2, offset).wait_send()
            turn(offset).wait_send()

    for offset in (0, *OFFSETS):

        @pl.when(jnp.logical_and(inside(here + offset), (here + offset) // 2 != column))
        def _(offset=offset):
            block_copy(offset).wait_send()


def fused(wavefunction, left_environment, operator_left, operator_right, right_environment, row_sector):
    ops, _ = schedule()
    vmem = pltpu.VMEM
    dma = pltpu.SemaphoreType.DMA
    count = len(MESSAGES)
    scratch = [
        vmem((192, 4, 384), BF16), vmem((1024, 3072), BF16), vmem((16, 192, 1536), BF16), vmem((16, 8, MAIN, 384), BF16),
        vmem((16, 8, REST, 384), BF16), vmem((1024, 1536), F32), vmem((512, 3072), BF16),
        vmem((512, 256), BF16), vmem((8, 512, 256), BF16), vmem((8, 512, 128), BF16),
        vmem((2, 3, 512, 256), BF16), vmem((2, 3, 512, 128), BF16),
        vmem((512, 256), F32), vmem((512, 128), F32), vmem((512, 256), BF16), vmem((512, 128), BF16),
        vmem((512, 256), BF16), vmem((512, 128), BF16),
        vmem((4, 128, 256), BF16), vmem((4, 128, 128), BF16), vmem((2, 3, 2, 128, 256), BF16),
        vmem((2, 3, 2, 128, 128), BF16), vmem((3, 128, 384), F32), vmem((2, 384, 128), F32),
        vmem((2, 384, 128), BF16), vmem((2, 384, 128), BF16), vmem((7, 128, 128), BF16),
        vmem((2, 8, 128, 128), BF16),
        dma((4,)), dma((count,)), dma((count,)), dma((24,)), dma((24,)), dma((16,)), dma((12,)),
        dma((2,)), dma((2,)), dma((12,)), dma((12,)), dma((6,)), dma((6,)), dma((7,)), dma((16,)),
    ]
    spec = pl.BlockSpec(memory_space=pl.ANY)
    return pl.pallas_call(
        functools.partial(kernel, ops),
        out_shape=(pltpu.VMEM((4, 128, 384), BF16), pltpu.VMEM((128, 256), F32)),
        in_specs=[spec] * 3 + [pl.BlockSpec(memory_space=pltpu.VMEM)] * 2
        + [pl.BlockSpec(memory_space=pltpu.SMEM)],
        out_specs=(pl.BlockSpec(memory_space=pltpu.VMEM),) * 2,
        scratch_shapes=scratch,
        compiler_params=pltpu.CompilerParams(
            collective_id=0, has_side_effects=True, vmem_limit_bytes=61 << 20
        ),
    )(
        wavefunction,
        left_environment.reshape(1024, 3072),
        right_environment.transpose(0, 2, 1),
        operator_left.transpose(0, 2, 3, 1),
        operator_right.transpose(0, 2, 3, 1),
        row_sector,
    )


def shards(
    wavefunction, left_environment, operator_left, operator_right, right_environment, row_sector
):
    raw, density = fused(
        wavefunction, left_environment, operator_left, operator_right, right_environment, row_sector
    )
    return raw.transpose(1, 0, 2), density


def solution(mesh):
    torus = Mesh(mesh.devices.reshape(2, 4, 2, 4, 2), AXES)
    in_specs = (P(LB, None, RB), P(None, LB, None), P(), P(), P(None, RB, LB), P())
    out_specs = (P(LB, None, RB), P(LB, RB))
    return jax.shard_map(
        shards, mesh=torus, in_specs=in_specs, out_specs=out_specs, check_vma=False
    )
```

```python
import functools
import math

import jax
import jax.numpy as jnp
from jax import lax
from jax.experimental import pallas as pl
from jax.experimental.pallas import tpu as pltpu
from jax.sharding import Mesh
from jax.sharding import PartitionSpec as P

BOND_WIDTH = 3072
SECTOR_TILES = 4
AXES = ("zl", "y", "core", "x", "zh")
LB = ("zl", "y", "core")
RB = ("x", "zh")
BF16, F32 = jnp.bfloat16, jnp.float32

MAIN, REST = 128, 64
PIECES = (
    (("z", 1, 0, 64), ("z", -1, 64, 48), ("y", 1, 112, 32), ("y", -1, 144, 48)),
    (("z", 1, 0, 32), ("z", -1, 32, 32), ("y", 1, 64, 32), ("y", -1, 96, 32)),
    (("z", 1, 0, 32), ("z", -1, 32, 16), ("y", -1, 48, 16)),
)
UNIT_BYTES = (1536 * 2, 8 * 384 * 2, 8 * 384 * 2)
SHARD = (192, MAIN, REST)
SOURCES = tuple((dz, dy) for dz in (0, 1) for dy in range(4))
MESSAGES = tuple(
    (phase, piece, source)
    for phase in range(3)
    for piece in range(len(PIECES[phase]))
    for source in SOURCES[1:]
)


FIRSTS = (((0, 0),), ((0, 1), (0, 3)), ((1, 0),), ((1, 1), (1, 3)), ((0, 2), (1, 2)))
LATER = (("away", 15.0), ("keep", 1.0), ("finish", 6.0), ("swap", 0.5), ("gram", 9.0))


def forwards(phase, piece, source):
    tree, turn = PIECES[phase][piece][:2]
    (dz, dy), on, back = source, "+-"[turn < 0], (-turn) % 4
    named = lambda link, place: (link, (phase, piece, place))
    if tree == "z":
        if source == (1, 0):
            return [named("+", (1, 3)), named("-", (1, 1))]
        return [named(on, (dz, 2))] if dy == back else []
    if dz:
        return []
    across = [named("z", (1, dy))]
    return [named(on, (0, 2)), *across] if dy == back else across


def own_sends():
    for phase in range(3):
        pieces = range(len(PIECES[phase]))
        for piece in sorted(pieces, key=lambda p: PIECES[phase][p][0] == "y"):
            yield "z", (phase, piece, (1, 0))
        for piece in sorted(pieces, key=lambda p: PIECES[phase][p][0] == "z"):
            yield "+", (phase, piece, (0, 3))
            yield "-", (phase, piece, (0, 1))


def schedule(rate=41e3, lag=3.0, lead=10.0, step=0.05):
    spent = (None, 1.1, 0.7)
    waiting = {link: [] for link in "+-z"}
    for order, (link, message) in enumerate(own_sends()):
        waiting[link].append((message[0], order, message, True))
    free_at = dict.fromkeys("+-z", 0.0)
    arriving, beside, done, ops, issued = [], [], set(), [], []
    pieces_left = {(p, s): len(PIECES[p]) for p in range(3) for s in SOURCES[1:]}
    ready = {(p, s): None for p in range(3) for s in SOURCES}
    for phase in range(3):
        ready[phase, (0, 0)] = 4.0 + phase
    firsts, mixes, seconds = 0, 0, [0, 0]
    later = []
    order, now, tc_free = 1000, 0.0, 0.0
    while seconds[1] < 8:
        now += step
        for link in "+-z":
            if free_at[link] <= now and waiting[link]:
                job = min(waiting[link])
                waiting[link].remove(job)
                phase, piece, _ = message = job[2]
                took = PIECES[phase][piece][3] * UNIT_BYTES[phase] / rate
                if job[3]:
                    issued.append((max(0.0, now - lead), len(issued), link, message))
                free_at[link] = now + took
                arriving.append((now + took + lag, message))
        if tc_free > now:
            continue
        landed = [entry for entry in arriving if entry[0] <= now]
        if landed:
            entry = min(landed)
            arriving.remove(entry)
            message = entry[1]
            onward = forwards(*message)
            for link, passed in onward:
                order += 1
                waiting[link].append((passed[0], order, passed, False))
            ops.append((now, "take", message, onward))
            phase, _, source = message
            pieces_left[phase, source] -= 1
            if not pieces_left[phase, source]:
                ops.append((now, "share", phase, source))
                size = SHARD[phase] * UNIT_BYTES[phase]
                ready[phase, source] = now + 2.0 + size / 400e3
            tc_free = now + 0.2
            continue
        able = [k for k, at in ready.items() if at is not None and at <= now and k not in done]
        group = FIRSTS[firsts] if firsts < len(FIRSTS) else None
        due = [entry for entry in later if entry[0] <= now]
        if due and due[0][1] == "first":
            later.remove(due[0])
            ops.append((now, *due[0][1:]))
            tc_free = now + 0.4 + 0.6 * len(due[0][2])
        elif group is not None:
            if all((0, source) in able for source in group):
                done.update((0, source) for source in group)
                for part in (0, 1):
                    later.append((now, "first", group, firsts == 0, part))
                firsts += 1
        elif mixes < 4:
            ops.append((now, "mix", mixes))
            mixes += 1
            tc_free = now + 1.1
        elif due:
            later.remove(due[0])
            ops.append((now, *due[0][1:]))
            tc_free = now + 0.7
        elif able:
            phase, source = min(able, key=lambda k: (k[0], ready[k]))
            done.add((phase, source))
            ops.append((now, "second", phase, source))
            seconds[phase - 1] += 1
            tc_free = now + spent[phase]
            if phase == 1 and seconds[0] == 8:
                wait = 0.0
                for name, gap in LATER:
                    wait += gap
                    later.append((tc_free + wait, name, 1))
    rest = [entry[1] for entry in later]
    ops += [(now, name, 1) for name in rest[:-1]]
    ops += [(now, name, 2) for name, _ in LATER[:-1]]
    ops += [(now, "gram", phase) for phase in ((1, 2) if rest else (2,))]
    for at, _, link, message in reversed(issued):
        place = next((i for i, op in enumerate(ops) if op[0] > at), len(ops))
        ops.insert(place, (at, "send", link, message))
    return [op[1:] for op in ops], now


OFFSETS = (1, 2, 3, -1, -2, -3)


def row_device(m):
    return {"zl": m // 8, "y": lax.rem(m // 2, 4), "core": lax.rem(m, 2)}


def column_device(n):
    return {"x": n // 2, "zh": lax.rem(n, 2)}


def inside(m):
    return jnp.logical_and(m >= 0, m < 16)


def ring(value, by, size):
    return lax.rem(value + (by % size), size)


def kernel(
    ops, w_ref, l_ref, r_ref, ol_ref, or_ref, sector_ref, out_ref, density_ref,
    raw, left, wide, main, rest, acc, mixed, coef, part_main, part_rest, from_main, from_rest,
    kept_main, kept_rest, away_main, away_rest, back_main, back_rest,
    tile_main, tile_rest, mates_main, mates_rest, grams, turned, turned_out, turned_in, blocks_out, blocks_in,
    local_sem, send_sem, recv_sem, share_send, share_recv, x_send, x_recv, z_send, z_recv,
    swap_send, swap_recv, turn_send, turn_recv, block_send, block_recv,
):
    zl, y, core, x, zh = (lax.axis_index(a) for a in AXES)
    gathered = (wide, main, rest)
    number = {m: i for i, m in enumerate(MESSAGES)}
    neighbour = {
        "+": {"y": ring(y, 1, 4)},
        "-": {"y": ring(y, -1, 4)},
        "z": {"zl": 1 - zl},
    }
    mesh_type = pl.DeviceIdType.MESH

    def chip(source):
        dz, dy = source
        return (1 - zl if dz else zl) * 4 + ring(y, dy, 4)

    barrier = pltpu.get_barrier_semaphore()
    here = chip((0, 0)) * 2 + core
    column = x * 2 + zh
    partners = [*neighbour.values(), {"core": 1 - core}]
    partners += [column_device(ring(column, by, 8)) for by in range(1, 8)]
    for partner in partners:
        pl.semaphore_signal(barrier, inc=1, device_id=partner, device_id_type=mesh_type)
    mates = jnp.int32(0)
    for offset in OFFSETS:
        mates += inside(here + offset).astype(jnp.int32)

        @pl.when(inside(here + offset))
        def _(offset=offset):
            pl.semaphore_signal(
                barrier, inc=1, device_id=row_device(here + offset), device_id_type=mesh_type
            )

    loads = [
        pltpu.make_async_copy(w_ref, raw, local_sem.at[0]),
        pltpu.make_async_copy(r_ref.at[:, 0:MAIN], main.at[here], local_sem.at[1]),
        pltpu.make_async_copy(r_ref.at[:, MAIN : MAIN + REST], rest.at[here], local_sem.at[2]),
        pltpu.make_async_copy(l_ref, left, local_sem.at[3]),
    ]
    for load in loads:
        load.start()
    loads[0].wait()
    wide[here] = raw[...].reshape(192, 1536)
    loads[1].wait()
    loads[2].wait()
    pl.semaphore_wait(barrier, len(partners) + mates)

    sent = []

    def piece_of(message, receiver):
        phase, piece, _ = message
        start, size = PIECES[phase][piece][2:]
        if phase == 0:
            return wide.at[receiver, pl.ds(start, size)]
        return gathered[phase].at[receiver, :, pl.ds(start, size)]

    def send(link, message, source):
        block = piece_of(message, chip(source) * 2 + core)
        at = number[message]
        copy = pltpu.make_async_remote_copy(
            block, block, send_sem.at[at], recv_sem.at[at],
            device_id=neighbour[link], device_id_type=mesh_type,
        )
        copy.start()
        sent.append(copy)

    def arrived(message):
        block = piece_of(message, chip(message[2]) * 2 + core)
        at = number[message]
        pltpu.make_async_remote_copy(
            block, block, send_sem.at[at], recv_sem.at[at],
            device_id=neighbour["z"], device_id_type=mesh_type,
        ).wait_recv()

    def share(phase, source, owner):
        at = phase * 8 + SOURCES.index(source)
        block = gathered[phase].at[chip(source) * 2 + owner]
        return pltpu.make_async_remote_copy(
            block, block, share_send.at[at], share_recv.at[at],
            device_id={"core": 1 - core}, device_id_type=mesh_type,
        )

    def coefficients():
        def of(size, dim):
            return lax.broadcasted_iota(jnp.int32, size, dim)

        def dot(a, b, dims=(((1,), (0,)), ((), ()))):
            return lax.dot_general(
                a, b, dims, precision=lax.Precision.HIGHEST, preferred_element_type=F32
            )

        across = (((1,), (1,)), ((), ()))
        tall, short = of((256, 32), 0), of((256, 32), 1)
        pick = (of((256, 8), 0) // 32 == of((256, 8), 1)).astype(F32)
        right = dot(pick, or_ref[...].reshape(32, 8), across)
        right = jnp.where(tall // 8 % 2 == short // 2 % 2, right, 0.0)
        i, j = of((32, 32), 0), of((32, 32), 1)
        right = dot(right, jnp.logical_and(i // 4 == j // 4, i % 2 == j % 2).astype(F32))
        right = jnp.where(tall // 16 % 2 == short // 2 % 2, right, 0.0)
        lefts = ol_ref[...].reshape(32, 8)
        total = None
        for site in (0, 1):
            wanted = jnp.logical_and(tall // 32 == short // 4, tall // 16 % 2 == short % 2)
            wanted = jnp.logical_and(wanted, short // 2 % 2 == site).astype(F32)
            i, j = of((8, 32), 0), of((8, 32), 1)
            place = jnp.logical_and(i == j // 4, j // 2 % 2 == site).astype(F32)
            term = dot(dot(wanted, lefts), place)
            total = term if total is None else total + term
        total = jnp.where(tall // 8 % 2 == short % 2, total, 0.0)
        full = dot(right, total, across)
        full = jnp.where(of((256, 256), 0) % 8 == of((256, 256), 1) % 8, full, 0.0)
        high = full.astype(BF16)
        coef[0:256] = high
        coef[256:512] = (full - high.astype(F32)).astype(BF16)

    def first(group, fresh, part):
        chips = [chip(source) for source in group]
        columns = [pl.ds(pl.multiple_of(k * 384, 384), 384) for k in chips]

        @pl.loop(part * 3, part * 3 + 3)
        def _(tile):
            lanes = pl.ds(pl.multiple_of(tile * 256, 256), 256)
            block = [wide[pl.ds(k * 2, 2), :, lanes].reshape(384, 256) for k in chips]
            rows = [left[:, c] for c in columns]
            product = jnp.dot(
                jnp.concatenate(rows, axis=1), jnp.concatenate(block, axis=0),
                preferred_element_type=F32,
            )
            if fresh:
                acc[:, lanes] = product
            else:
                acc[:, lanes] += product

    def mix(quarter):
        @pl.loop(quarter * 2, quarter * 2 + 2)
        def _(group):
            halves = []
            for sub in range(2):
                start = pl.multiple_of(group * 16 + sub * 8, 8)
                stack = jnp.concatenate(
                    [
                        acc[pl.ds(a * 128 + start, 8), s * 384 : s * 384 + 384]
                        for a in range(8)
                        for s in range(4)
                    ],
                    axis=0,
                )
                top = stack.astype(BF16)
                under = (stack - top.astype(F32)).astype(BF16)
                both = jnp.dot(coef[...], top, preferred_element_type=F32)
                third = jnp.dot(coef[0:256], under, preferred_element_type=F32)
                halves.append(both[0:256] + both[256:512] + third)
            for v in range(8):
                for out_site in range(4):
                    at = (v * 4 + out_site) * 8
                    value = jnp.concatenate([h[at : at + 8] for h in halves], axis=0)
                    rows = pl.ds(pl.multiple_of(out_site * 128 + group * 16, 16), 16)
                    mixed[rows, v * 384 : v * 384 + 384] = value.astype(BF16)

    parts, froms = (None, part_main, part_rest), (None, from_main, from_rest)
    keeps, aways, backs = (None, kept_main, kept_rest), (None, away_main, away_rest), (None, back_main, back_rest)

    def to_owner(phase, k):
        owner, half = k // 2, lax.rem(k, 2)
        slot = lax.rem(x - owner + 7, 4)
        slot = jnp.minimum(slot, 2)
        copy = pltpu.make_async_remote_copy(
            parts[phase].at[k], froms[phase].at[half, slot],
            x_send.at[(phase - 1) * 8 + k], x_recv.at[(phase - 1) * 6 + half * 3 + slot],
            device_id={"x": owner}, device_id_type=mesh_type,
        )
        return copy, x != owner

    def second(phase, source):
        k = chip(source)
        width = 2 * SHARD[phase]

        total = None
        for v in range(0, 8, 2):
            block = [gathered[phase][pl.ds(k * 2, 2), v + j].reshape(width, 384) for j in (0, 1)]
            product = lax.dot_general(
                mixed[:, v * 384 : v * 384 + 768], jnp.concatenate(block, axis=1),
                (((1,), (1,)), ((), ())), preferred_element_type=F32,
            )
            total = product if total is None else total + product
        parts[phase][k] = total.astype(BF16)

        copy, away = to_owner(phase, k)

        @pl.when(away)
        def _():
            copy.start()

    def z_copy(phase):
        return pltpu.make_async_remote_copy(
            aways[phase], backs[phase], z_send.at[phase - 1], z_recv.at[phase - 1],
            device_id={"zh": 1 - zh}, device_id_type=mesh_type,
        )

    def sum_x(phase, half, put):
        for slot in range(3):
            pltpu.make_async_remote_copy(
                parts[phase].at[0], froms[phase].at[half, slot],
                x_send.at[0], x_recv.at[(phase - 1) * 6 + half * 3 + slot],
                device_id={"x": ring(x, 1, 4)}, device_id_type=mesh_type,
            ).wait_recv()

        @pl.loop(0, 8)
        def _(tile):
            rows = pl.ds(pl.multiple_of(tile * 64, 64), 64)
            total = parts[phase][x * 2 + half, rows].astype(F32)
            for slot in range(3):
                total += froms[phase][half, slot, rows].astype(F32)
            put(rows, total)

    def sum_away(phase):
        def put(rows, total):
            aways[phase][rows] = total.astype(BF16)

        sum_x(phase, 1 - zh, put)
        z_copy(phase).start()

    def sum_keep(phase):
        def put(rows, total):
            keeps[phase][rows] = total

        sum_x(phase, zh, put)

    tiles = (None, tile_main, tile_rest)
    mates_of = (None, mates_main, mates_rest)

    def finish(phase):
        z_copy(phase).wait_recv()
        for site in range(4):
            rows = slice(site * 128, site * 128 + 128)
            value = keeps[phase][rows] + backs[phase][rows].astype(F32)
            keeps[phase][rows] = value
            tiles[phase][site] = value.astype(BF16)

    def swap(phase, offset):
        half, at = int(offset > 0), abs(offset) - 1
        slot = ((phase - 1) * 2 + half) * 3 + at
        return pltpu.make_async_remote_copy(
            tiles[phase].at[pl.ds(half * 2, 2)], mates_of[phase].at[half, at],
            swap_send.at[slot], swap_recv.at[slot],
            device_id=row_device(here + offset), device_id_type=mesh_type,
        )

    def nt(a, b):
        return lax.dot_general(a, b, (((1,), (1,)), ((), ())), preferred_element_type=F32)

    def swaps(phase):
        for offset in OFFSETS:

            @pl.when(inside(here + offset))
            def _(offset=offset):
                swap(phase, offset).start()

        tile = jnp.concatenate([tiles[phase][site] for site in range(4)], axis=1)
        own = nt(tile, tile)
        grams[2, :, 0:128] = own if phase == 1 else grams[2, :, 0:128] + own

    def gram(phase):
        width = 2 * SHARD[phase]
        for half in (0, 1):
            for offset in OFFSETS[3 - 3 * half :][:3]:

                @pl.when(inside(here - offset))
                def _(offset=offset):
                    swap(phase, offset).wait_recv()

            mine = jnp.concatenate([tiles[phase][half * 2 + j] for j in (0, 1)], axis=1)
            theirs = [mates_of[phase][half, :, j].reshape(384, width) for j in (0, 1)]
            theirs = jnp.concatenate(theirs, axis=1)
            straight, crossed = nt(mine, theirs), nt(theirs, mine)
            if phase == 1:
                grams[half] = straight
                turned[half] = crossed
            else:
                turned_out[half] = (turned[half] + crossed).astype(BF16)
                grams[half] += straight
                for offset in OFFSETS[3 * half :][:3]:

                    @pl.when(inside(here + offset))
                    def _(offset=offset):
                        turn(offset).start()

    def turn(offset):
        half, at = int(offset < 0), abs(offset) - 1
        return pltpu.make_async_remote_copy(
            turned_out.at[half, pl.ds(at * 128, 128)], turned_in.at[1 - half, pl.ds(at * 128, 128)],
            turn_send.at[half * 3 + at], turn_recv.at[half * 3 + at],
            device_id=row_device(here + offset), device_id_type=mesh_type,
        )

    def block_copy(offset):
        mate = here + offset
        owner, half = mate // 2, lax.rem(mate, 2)
        return pltpu.make_async_remote_copy(
            blocks_out.at[offset + 3], blocks_in.at[half, column],
            block_send.at[offset + 3], block_recv.at[half * 8 + column],
            device_id=column_device(owner), device_id_type=mesh_type,
        )

    def reach():
        for offset in (0, *OFFSETS[3:], *OFFSETS[:3]):
            half, at = int(offset < 0), abs(offset) - 1

            @pl.when(inside(here + offset))
            def _(offset=offset, half=half, at=at):
                if offset:
                    turn(-offset).wait_recv()
                    came = turned_in[half, at * 128 : at * 128 + 128].astype(F32)
                    value = grams[half, :, at * 128 : at * 128 + 128] + came
                else:
                    value = grams[2, :, 0:128]
                owner = (here + offset) // 2

                @pl.when(owner == column)
                def _():
                    blocks_in[lax.rem(here + offset, 2), column] = value.astype(BF16)

                @pl.when(owner != column)
                def _():
                    blocks_out[offset + 3] = value.astype(BF16)
                    block_copy(offset).start()

        for half in (0, 1):
            mate = column * 2 + half
            near = jnp.logical_and(mate - here <= 3, here - mate <= 3)
            lanes = slice(half * 128, half * 128 + 128)

            @pl.when(near)
            def _(half=half, mate=mate, lanes=lanes):
                for by in range(1, 8):
                    source = ring(column, by, 8)
                    pltpu.make_async_remote_copy(
                        blocks_out.at[0], blocks_in.at[half, source],
                        block_send.at[0], block_recv.at[half * 8 + source],
                        device_id=column_device(source), device_id_type=mesh_type,
                    ).wait_recv()
                total = sum(blocks_in[half, n].astype(F32) for n in range(8))
                same_sector = sector_ref[mate] == sector_ref[here]
                total = total * (1.0 / math.sqrt(4.0 * BOND_WIDTH))
                density_ref[:, lanes] = jnp.where(same_sector, total, 0.0)

            @pl.when(jnp.logical_not(near))
            def _(lanes=lanes):
                density_ref[:, lanes] = jnp.zeros((128, 128), F32)

    def write_out():
        lane = lax.broadcasted_iota(jnp.int32, (128, 128), 1)
        for site in range(4):
            rows = slice(site * 128, site * 128 + 128)
            out_ref[site, :, 0:128] = tile_main[site, :, 0:128]
            rolled = pltpu.roll(kept_main[rows, 128:256], 64, 1)
            last = kept_rest[rows, :]
            out_ref[site, :, 128:256] = jnp.where(lane < 64, last, rolled).astype(BF16)
            out_ref[site, :, 256:384] = jnp.where(lane < 64, rolled, last).astype(BF16)

    after = dict(away=sum_away, keep=sum_keep, finish=finish, swap=swaps, gram=gram)
    for phase in range(3):
        share(phase, (0, 0), core).start()
    for op in ops:
        if op[0] == "first" and op[2] and not op[3]:
            coefficients()
        if op[0] == "send":
            send(op[1], op[2], (0, 0))
        elif op[0] == "take":
            arrived(op[1])
            for link, passed in op[2]:
                send(link, passed, op[1][2])
        elif op[0] == "share":
            share(op[1], op[2], core).start()
        elif op[0] == "first":
            if not op[3]:
                for source in op[1]:
                    share(0, source, 1 - core).wait_recv()
            if op[2] and not op[3]:
                loads[3].wait()
            first(*op[1:])
        elif op[0] == "mix":
            mix(op[1])
        elif op[0] == "second":
            share(op[1], op[2], 1 - core).wait_recv()
            second(op[1], op[2])
        else:
            if op == ("gram", 2):
                write_out()
            after[op[0]](op[1])
    reach()
    for copy in sent:
        copy.wait_send()
    for phase in range(3):
        for source in SOURCES:
            share(phase, source, core).wait_send()
    for phase in (1, 2):
        z_copy(phase).wait_send()
        for k in range(8):
            copy, away = to_owner(phase, k)

            @pl.when(away)
            def _(copy=copy):
                copy.wait_send()

    for offset in OFFSETS:

        @pl.when(inside(here + offset))
        def _(offset=offset):
            swap(1, offset).wait_send()
            swap(2, offset).wait_send()
            turn(offset).wait_send()

    for offset in (0, *OFFSETS):

        @pl.when(jnp.logical_and(inside(here + offset), (here + offset) // 2 != column))
        def _(offset=offset):
            block_copy(offset).wait_send()


def fused(wavefunction, left_environment, operator_left, operator_right, right_environment, row_sector):
    ops, _ = schedule()
    vmem = pltpu.VMEM
    dma = pltpu.SemaphoreType.DMA
    count = len(MESSAGES)
    scratch = [
        vmem((192, 4, 384), BF16), vmem((1024, 3072), BF16), vmem((16, 192, 1536), BF16), vmem((16, 8, MAIN, 384), BF16),
        vmem((16, 8, REST, 384), BF16), vmem((1024, 1536), F32), vmem((512, 3072), BF16),
        vmem((512, 256), BF16), vmem((8, 512, 256), BF16), vmem((8, 512, 128), BF16),
        vmem((2, 3, 512, 256), BF16), vmem((2, 3, 512, 128), BF16),
        vmem((512, 256), F32), vmem((512, 128), F32), vmem((512, 256), BF16), vmem((512, 128), BF16),
        vmem((512, 256), BF16), vmem((512, 128), BF16),
        vmem((4, 128, 256), BF16), vmem((4, 128, 128), BF16), vmem((2, 3, 2, 128, 256), BF16),
        vmem((2, 3, 2, 128, 128), BF16), vmem((3, 128, 384), F32), vmem((2, 384, 128), F32),
        vmem((2, 384, 128), BF16), vmem((2, 384, 128), BF16), vmem((7, 128, 128), BF16),
        vmem((2, 8, 128, 128), BF16),
        dma((4,)), dma((count,)), dma((count,)), dma((24,)), dma((24,)), dma((16,)), dma((12,)),
        dma((2,)), dma((2,)), dma((12,)), dma((12,)), dma((6,)), dma((6,)), dma((7,)), dma((16,)),
    ]
    spec = pl.BlockSpec(memory_space=pl.ANY)
    return pl.pallas_call(
        functools.partial(kernel, ops),
        out_shape=(pltpu.VMEM((4, 128, 384), BF16), pltpu.VMEM((128, 256), F32)),
        in_specs=[spec] * 3 + [pl.BlockSpec(memory_space=pltpu.VMEM)] * 2
        + [pl.BlockSpec(memory_space=pltpu.SMEM)],
        out_specs=(pl.BlockSpec(memory_space=pltpu.VMEM),) * 2,
        scratch_shapes=scratch,
        compiler_params=pltpu.CompilerParams(
            collective_id=0, has_side_effects=True, vmem_limit_bytes=61 << 20
        ),
    )(
        wavefunction,
        left_environment.reshape(1024, 3072),
        right_environment.transpose(0, 2, 1),
        operator_left.transpose(0, 2, 3, 1),
        operator_right.transpose(0, 2, 3, 1),
        row_sector,
    )


def shards(
    wavefunction, left_environment, operator_left, operator_right, right_environment, row_sector
):
    raw, density = fused(
        wavefunction, left_environment, operator_left, operator_right, right_environment, row_sector
    )
    return raw.transpose(1, 0, 2), density


def solution(mesh):
    torus = Mesh(mesh.devices.reshape(2, 4, 2, 4, 2), AXES)
    in_specs = (P(LB, None, RB), P(None, LB, None), P(), P(), P(None, RB, LB), P())
    out_specs = (P(LB, None, RB), P(LB, RB))
    return jax.shard_map(
        shards, mesh=torus, in_specs=in_specs, out_specs=out_specs, check_vma=False
    )
```
